256 devices in a mesh: region: 8 (over y, core), gy: 8 (over z), gz: 4 (over x).
Axes of the slice: x: 4, y: 4, z: 8, core: 2. Of those that a mesh axis runs over, the one named last changes fastest.
Arguments:
- loads: float32 [256, 32, 768], P(('region', 'gy', 'gz')), may hold values from -62 to 62
- schur: bfloat16 [256, 768, 768], P(('region', 'gy', 'gz')), may hold values from -1 to 3.5, as said below
- dirichlet: bfloat16 [256, 768, 768], P(('region', 'gy', 'gz')), may hold values from -1 to 1.75, as said below
- coupling: bfloat16 [256, 768, 128], P(('region', 'gy', 'gz')), may hold values from -0.21875 to 0.21875
- coarse_inverse: float32 [512, 512], replicated, may hold values from -1 to 1, as said below
- pairing: int32 [256, 6, 128], P(('region', 'gy', 'gz')), may hold values from 0 to 127, as said below
- corner_map: int32 [256, 128], P(('region', 'gy', 'gz')), may hold values from 0 to 511, as said below
- counts: int32 [256], P(('region', 'gy', 'gz')), may hold values from 1 to 1, as said below
Outputs:
- solution: float32 [256, 32, 768], P(('region', 'gy', 'gz'))
- residual: float32 [256, 32, 768], P(('region', 'gy', 'gz'))
The draws below stay inside these ranges and needn't reach their ends.
Inputs may be any that keep to these rules, and one draw needn't show every extreme that they name: `schur`: symmetric and positive definite for every subdomain. `dirichlet`: symmetric and positive definite for every subdomain. `coarse_inverse`: symmetric and positive definite. `counts`: some device has all 1 slots live. `pairing`: within each face block a permutation; the two slots that hold one multiplier name each other. `corner_map`: device d owns coarse degrees of freedom d * 2 to d * 2 + 1; every corner of a subdomain on device d maps to one owned by d or by a device one step away along one of the three directions; slot 0 of device d maps its first 2 corners to d's own in order.
All inputs are finite; a program needn't handle non-finite values.
Results may differ from the reference program's by a relative error of at most 0.0065.
The reference program's roundings to bfloat16 on the way count: a program that leaves them out, or rounds other values in their place, can miss the bound.
Values sent between devices are 32-bit elements; how exact they have to be, the bound alone decides.
No kernel may reach another device: no remote copies, remote signals or barrier semaphores. Data moves between devices by JAX's collectives and lax.ppermute only.
A program may use at most 64 MiB of HBM per device.

```python
import jax
import jax.numpy as jnp
import numpy as np
from jax import lax

SUB_DEV = 1
FACE = 128
LOADS = 32
CORNERS = 128
CORN_DEV = 2
ITERS = 2
MULT = 768
SUBS = 256
COARSE = 512
REGIONS = 8
TILE_Y = 8
TILE_Z = 4


def definite_blocks(key, number, order, low, high, scale):

    def single(sub_key):
        diag_key, off_key = jax.random.split(sub_key)
        diagonal = jax.random.uniform(diag_key, (order,), jnp.float32, low, high)
        raw_part = jax.random.uniform(off_key, (order, order), jnp.float32, -1.0, 1.0)
        symmetric = (raw_part + raw_part.T) * (0.5 / order ** 0.5)
        identity = jnp.eye(order, dtype=jnp.float32)
        return (symmetric * (1.0 - identity) + diagonal[:, None] * identity) * scale
    return lax.map(single, jax.random.split(key, number))


def draw_schur(key, part):
    key = jax.random.fold_in(key, 3)
    return definite_blocks(key, SUBS, MULT, 1.5, 3.0, 1.0).astype(jnp.bfloat16)


def draw_dirichlet(key, part):
    key = jax.random.fold_in(key, 4)
    return definite_blocks(key, SUBS, MULT, 1.5, 3.0, 0.5).astype(jnp.bfloat16)


def draw_coarse_inverse(key, part):
    key = jax.random.fold_in(key, 6)
    factor = (CORN_DEV / (SUB_DEV * CORNERS)) ** 0.5
    return definite_blocks(key, 1, COARSE, 1.5, 3.0, factor)[0]


def draw_loads(key, part):
    key = jax.random.fold_in(key, 7)
    base_key, sub_key, col_key = jax.random.split(key, 3)
    devices = SUBS // SUB_DEV
    position = (jnp.arange(SUBS) // SUB_DEV).astype(jnp.float32) / max(devices - 1, 1)
    base = jnp.clip(jax.random.normal(base_key, (SUBS, LOADS, MULT), jnp.float32), -5.0, 5.0)
    ramp = jnp.exp(jnp.log(3.0) * position)
    sub_scale = jnp.exp(jax.random.uniform(sub_key, (SUBS, 1, 1), jnp.float32, 0.0, jnp.log(4.0)))
    col_scale = jnp.exp(jax.random.uniform(col_key, (1, LOADS, 1), jnp.float32, 0.0, jnp.log(3.0)))
    return base * ramp[:, None, None] * sub_scale * col_scale / 3.0


def draw_pairing(key, part):
    key = jax.random.fold_in(key, 9)
    global_ids = jnp.arange(SUBS)
    strides = [TILE_Y * TILE_Z * SUB_DEV, TILE_Z * SUB_DEV, 1]
    blocks = []
    for dimension in range(3):
        axis_key = jax.random.fold_in(key, dimension)

        def permute(number, axis_key=axis_key):
            return jax.random.permutation(jax.random.fold_in(axis_key, number), FACE)
        upper_side = jax.vmap(permute)(global_ids)
        lower_side = jax.vmap(permute)(jnp.clip(global_ids - strides[dimension], 0, SUBS - 1))
        blocks.append(jnp.argsort(lower_side, axis=1, stable=True))
        blocks.append(upper_side)
    return jnp.stack(blocks, axis=1).astype(jnp.int32)


def draw_corner_map(key, part):
    key = jax.random.fold_in(key, 11)
    pick_key, own_key = jax.random.split(key)
    device_of = jnp.arange(SUBS, dtype=jnp.int32) // SUB_DEV
    first = device_of // (TILE_Y * TILE_Z)
    second = device_of // TILE_Z % TILE_Y
    third = device_of % TILE_Z
    offsets = jnp.asarray(np.array([[0, 0, 0], [1, 0, 0], [-1, 0, 0], [0, 1, 0], [0, -1, 0], [0, 0, 1], [0, 0, -1]], dtype=np.int32))
    choose = jax.random.randint(pick_key, (SUBS, CORNERS), 0, 7)
    moved = offsets[choose]
    near_a = jnp.clip(first[:, None] + moved[:, :, 0], 0, REGIONS - 1)
    near_b = jnp.clip(second[:, None] + moved[:, :, 1], 0, TILE_Y - 1)
    near_c = jnp.clip(third[:, None] + moved[:, :, 2], 0, TILE_Z - 1)
    near_dev = (near_a * TILE_Y + near_b) * TILE_Z + near_c
    which = jax.random.randint(own_key, (SUBS, CORNERS), 0, CORN_DEV)
    ids = near_dev * CORN_DEV + which
    corner_ids = jnp.arange(CORNERS, dtype=jnp.int32)
    forced = (jnp.arange(SUBS) % SUB_DEV == 0)[:, None] & (corner_ids < CORN_DEV)[None, :]
    own = device_of[:, None] * CORN_DEV + corner_ids[None, :]
    return jnp.where(forced, own, ids).astype(jnp.int32)


def draw_counts(key, part):
    key = jax.random.fold_in(key, 5)
    value_key, top_key = jax.random.split(key)
    devices = SUBS // SUB_DEV
    values = jax.random.randint(value_key, (devices,), 1, SUB_DEV + 1)
    fullest = jax.random.randint(top_key, (), 0, devices)
    return values.at[fullest].set(SUB_DEV).astype(jnp.int32)


def levels(key, extent, shards, least, high):
    def one(dim, shards_of):
        draws = jax.random.uniform(jax.random.fold_in(jax.random.fold_in(key, 6), dim), (shards_of,), jnp.float32, least / len(shards), high / len(shards))
        return jnp.repeat(jnp.exp(draws), extent[dim] // shards_of).reshape((-1,) + (1,) * (len(extent) - dim - 1))

    gain = one(*shards[0])
    for cut in shards[1:]:
        gain = gain * one(*cut)
    return gain


def centred(key, dims, scale, most, shards=(), kind=jnp.bfloat16):
    result = jax.random.normal(key, dims, jnp.float32) * scale
    if len(shards) > 0:
        result = levels(key, dims, shards, -0.22, 0.18) * result
    return jnp.clip(result, min=-most, max=most).astype(kind)


def setup_inputs(seed: int = 0) -> dict:
    key_of = jax.random.split(jax.random.key(seed), 9)
    loads = draw_loads(jax.random.fold_in(key_of[8], 71), 0)
    schur = draw_schur(jax.random.fold_in(key_of[8], 71), 0)
    dirichlet = draw_dirichlet(jax.random.fold_in(key_of[8], 71), 0)
    coupling = centred(key_of[3], (SUBS, MULT, CORNERS), MULT ** -0.5, 0.21875, ((0, 256),))
    coarse_inverse = draw_coarse_inverse(jax.random.fold_in(key_of[8], 71), 0)
    pairing = draw_pairing(jax.random.fold_in(key_of[8], 71), 0)
    corner_map = draw_corner_map(jax.random.fold_in(key_of[8], 71), 0)
    counts = draw_counts(jax.random.fold_in(key_of[8], 71), 0)
    return dict(loads=loads, schur=schur, dirichlet=dirichlet, coupling=coupling, coarse_inverse=coarse_inverse, pairing=pairing, corner_map=corner_map, counts=counts)


HIGHEST_PREC = lax.Precision.HIGHEST


def shifted(block, dimension, offset):
    length = block.shape[dimension]
    widths = [(1, 1) if position == dimension else (0, 0) for position in range(block.ndim)]
    padded = jnp.pad(block, widths)
    return lax.slice_in_dim(padded, 1 - offset, 1 - offset + length, axis=dimension)


def partner_values(values, pairing):
    columns = values.shape[1]
    grid = values.reshape(REGIONS, TILE_Y, TILE_Z * SUB_DEV, columns, 6, FACE)
    pieces = []
    for dimension in range(3):
        pieces.append(shifted(grid[:, :, :, :, 2 * dimension + 1], dimension, 1))
        pieces.append(shifted(grid[:, :, :, :, 2 * dimension], dimension, -1))
    received = jnp.stack(pieces, axis=4).reshape(SUBS, columns, 6, FACE)
    indices = jnp.broadcast_to(pairing[:, None, :, :], received.shape)
    return jnp.take_along_axis(received, indices, axis=3).reshape(SUBS, columns, MULT)


def assemble(values, living, pairing):
    return living[:, None, None] * (values + partner_values(values, pairing))


def weighted_inner(weight, left, right_vec):
    return jnp.sum(weight * left * right_vec, axis=(0, 2))


def block_product(vectors, matrices):
    return lax.map(lambda operands: jnp.dot(operands[0], operands[1], preferred_element_type=jnp.float32), (vectors, matrices))


def reference(loads, schur, dirichlet, coupling, coarse_inverse, pairing, corner_map, counts):
    slot_ids = jnp.arange(SUB_DEV, dtype=jnp.int32)
    living = (slot_ids[None, :] < counts[:, None]).reshape(SUBS).astype(jnp.float32)
    live_col = living[:, None, None]
    live_ones = jnp.broadcast_to(live_col, (SUBS, 1, MULT))
    multiplicity = assemble(live_ones, living, pairing)
    weight = live_col / jnp.maximum(multiplicity, 1.0)
    right_side = assemble(loads * live_col, living, pairing)

    def precondition(residual):
        scaled = (weight * residual).astype(jnp.bfloat16)
        return assemble(weight * block_product(scaled, dirichlet), living, pairing)

    def operator(direction):
        dir_bf = direction.astype(jnp.bfloat16)
        local_terms = block_product(dir_bf, schur)
        corner_terms = block_product(dir_bf, coupling) * live_col
        flat_terms = jnp.swapaxes(corner_terms, 1, 2).reshape(SUBS * CORNERS, LOADS)
        gathered = jax.ops.segment_sum(flat_terms, corner_map.reshape(-1), num_segments=COARSE)
        solved = jnp.dot(coarse_inverse, gathered, precision=HIGHEST_PREC).astype(jnp.bfloat16)
        picked = solved[corner_map]
        coarse_terms = lax.map(lambda operands: jnp.dot(jnp.transpose(operands[0]), jnp.transpose(operands[1]), preferred_element_type=jnp.float32), (picked, coupling))
        return assemble(live_col * (local_terms + coarse_terms), living, pairing)

    residual = right_side
    solution = jnp.zeros_like(right_side)
    precond = precondition(residual)
    resid_dot = weighted_inner(weight, residual, precond)
    direction = precond
    for iteration in range(ITERS):
        image_vec = operator(direction)
        step_size = (resid_dot / weighted_inner(weight, direction, image_vec))[None, :, None]
        solution = solution + step_size * direction
        residual = residual - step_size * image_vec
        if iteration + 1 < ITERS:
            precond = precondition(residual)
            new_dot = weighted_inner(weight, residual, precond)
            direction = precond + (new_dot / resid_dot)[None, :, None] * direction
            resid_dot = new_dot
    return solution, residual
```

```python
import jax
import jax.numpy as jnp
from jax import lax
from jax.experimental import pallas as pl
from jax.experimental.pallas import tpu as pltpu
from jax.sharding import PartitionSpec as P

AXES = ("region", "gy", "gz")
SIZES = (8, 8, 4)
F32 = jnp.float32
BF16 = jnp.bfloat16
LOADS = 32
FACE = 128
MULT = 768
COARSE = 512
SIDE = 32
HIGHEST = lax.Precision.HIGHEST
VM = pl.BlockSpec(memory_space=pltpu.VMEM)
SM = pl.BlockSpec(memory_space=pltpu.SMEM)


def matmul(left, right):
    return jnp.dot(left, right, preferred_element_type=F32)


def matmul_nt(left, right, precision=None):
    return lax.dot_general(
        left, right, (((1,), (1,)), ((), ())), precision=precision, preferred_element_type=F32
    )


def live_of(counts):
    return (counts[0] > 0).astype(F32)


def coords():
    return [lax.axis_index(axis) for axis in AXES]


def store_sends(sends, faces):
    for e, place in enumerate(coords()):
        odd = place % 2 == 1
        sends[2 * e][...] = jnp.where(odd, faces[2 * e], faces[2 * e + 1])
        sends[2 * e + 1][...] = jnp.where(odd, faces[2 * e + 1], faces[2 * e])


def received_faces(recvs, rows):
    out = []
    for e, place in enumerate(coords()):
        odd = place % 2 == 1
        first, second = recvs[2 * e][rows, :], recvs[2 * e + 1][rows, :]
        lower = jnp.where(odd, first, second)
        upper = jnp.where(odd, second, first)
        out.append(jnp.where(place > 0, lower, 0.0))
        out.append(jnp.where(place < SIZES[e] - 1, upper, 0.0))
    return out


def partner(recvs, pairing, rows=slice(0, LOADS)):
    faces = received_faces(recvs, rows)
    parts = []
    for f in range(6):
        index = jnp.broadcast_to(pairing[0, f : f + 1, :], faces[f].shape)
        parts.append(jnp.take_along_axis(faces[f], index, axis=1))
    return jnp.concatenate(parts, axis=1)


def split_faces(value):
    return [value[:, f * FACE : (f + 1) * FACE] for f in range(6)]


def load_sums(left, right):
    return matmul_nt(jnp.ones((8, MULT), F32), left * right, HIGHEST)


def column(row):
    r = lax.broadcasted_iota(jnp.int32, (LOADS, LOADS), 0)
    c = lax.broadcasted_iota(jnp.int32, (LOADS, LOADS), 1)
    return jnp.sum(jnp.where(r == c, row, 0.0), axis=1, keepdims=True)


def prepare_kernel(counts, loads, *sends):
    live = live_of(counts)
    value = loads[0] * live
    mark = jnp.full((8, FACE), live, F32)
    faces = [jnp.concatenate([face, mark], axis=0) for face in split_faces(value)]
    store_sends(sends, faces)


def precondition(weight, residual, dirichlet):
    scaled = (weight * residual).astype(BF16)
    return weight * matmul(scaled, dirichlet[0])


def first_kernel(counts, loads, pairing, dirichlet, *refs):
    recvs, (resid, weight_ref, terms, dots), sends = refs[:6], refs[6:10], refs[10:]
    live = live_of(counts)
    residual = live * (loads[0] * live + partner(recvs, pairing))
    multiplicity = live * (live + partner(recvs, pairing, slice(LOADS, LOADS + 8)))
    weight = live / jnp.maximum(multiplicity, 1.0)
    weight_ref[...] = weight
    resid[...] = residual
    applied = precondition(weight[0:1], residual, dirichlet)
    terms[...] = applied
    dots[...] = load_sums(residual, applied)
    store_sends(sends, split_faces(applied))


def corner_message(corner_map, corner_terms, scalars):
    place = coords()
    devices = []
    for step in ((0, 0, 0), (1, 0, 0), (-1, 0, 0), None, (0, 1, 0), (0, -1, 0), (0, 0, 1), (0, 0, -1)):
        if step is None:
            devices.append(None)
            continue
        a, b, c = [(p + s + n) % n for p, s, n in zip(place, step, SIZES)]
        devices.append((a * SIZES[1] + b) * SIZES[2] + c)
    row = lax.broadcasted_iota(jnp.int32, (16, FACE), 0)
    target = jnp.full((16, FACE), -1, jnp.int32)
    for index, device in enumerate(devices):
        for which in range(2):
            at = which * 8 + (index % 2) * 4 + index // 2
            if device is not None:
                target = jnp.where(row == at, device * 2 + which, target)
    chosen = (target == corner_map[0:1, :]).astype(F32)
    sums = matmul_nt(chosen, corner_terms, HIGHEST)
    body = jnp.concatenate([sums[0:4], sums[8:12], sums[4:8], sums[12:16]], axis=1)
    zero = jnp.zeros((1, LOADS), F32)
    tail = jnp.concatenate(list(scalars) + [zero] * (4 - len(scalars)), axis=1)
    return jnp.concatenate([body, jnp.broadcast_to(tail, (4, FACE))], axis=0)


def send_message(out, message):
    for peer in range(out.shape[0]):
        out[peer] = message


def second_kernel(counts, pairing, corner_map, schur, coupling, terms, dots, *refs):
    recvs, (z_ref, local_ref, out) = refs[:6], refs[6:]
    live = live_of(counts)
    direction = live * (terms[...] + partner(recvs, pairing))
    dir_bf = direction.astype(BF16)
    local_terms = live * matmul(dir_bf, schur[0])
    corner_terms = live * matmul(dir_bf, coupling[0])
    z_ref[...] = direction
    local_ref[...] = local_terms
    curve = load_sums(direction, local_terms)
    send_message(out, corner_message(corner_map, corner_terms, (dots[0:1], curve[0:1])))


def plane_kernel(got, out):
    rows = lax.broadcasted_iota(jnp.int32, (SIDE, FACE), 0) % SIZES[2]
    lane = lax.broadcasted_iota(jnp.int32, (SIDE, FACE), 1)
    along_b = got[:, 2, :]
    along_c = got[:, 3, :]
    b_up = pltpu.roll(along_b, SIZES[2], 0)
    b_down = pltpu.roll(pltpu.roll(along_b, SIDE - SIZES[2], 0), 64, 1)
    c_up = jnp.where(rows == 0, pltpu.roll(along_c, SIDE - 3, 0), pltpu.roll(along_c, 1, 0))
    c_down = jnp.where(rows == 3, pltpu.roll(along_c, 3, 0), pltpu.roll(along_c, SIDE - 1, 0))
    c_down = pltpu.roll(c_down, 64, 1)
    own = got[:, 0, :] + jnp.where(lane < 64, (b_up + b_down) + (c_up + c_down), 0.0)
    down = got[:, 1, :]
    scalars = jnp.broadcast_to(jnp.sum(got[:, 4, :], axis=0, keepdims=True), (8, FACE))
    for peer in range(SIZES[0]):
        out[peer, 0:32, :] = own
        out[peer, 32:64, :] = down
        out[peer, 64:72, :] = scalars


def coarse_sums(got, scratch):
    pieces = []
    for a in range(SIZES[0]):
        below, above = (a + 7) % 8, (a + 1) % 8
        pieces.append(
            got[a, 0:32, :] + pltpu.roll(got[below, 0:32, :], 64, 1) + got[above, 32:64, :]
        )
    whole = jnp.concatenate(pieces, axis=0)
    scratch[pl.Slice(0, COARSE // 2, 2), :] = whole[:, 0:32]
    scratch[pl.Slice(1, COARSE // 2, 2), :] = whole[:, 32:64]
    scalars = got[0, 64:72, :]
    for a in range(1, SIZES[0]):
        scalars = scalars + got[a, 64:72, :]
    return scratch[...], [scalars[0:1, i * 32 : i * 32 + 32] for i in range(4)]


def coarse_solve(inverse, gathered, corner_map, coupling):
    solved = jnp.dot(
        inverse[...], gathered, precision=HIGHEST, preferred_element_type=F32
    ).astype(BF16)
    row = lax.broadcasted_iota(jnp.int32, (COARSE, FACE), 0)
    chosen = (row == corner_map[0:1, :]).astype(F32).astype(BF16)
    picked = lax.dot_general(
        solved, chosen, (((0,), (0,)), ((), ())), preferred_element_type=F32
    ).astype(BF16)
    energy = jnp.sum(solved.astype(F32) * gathered, axis=0, keepdims=True)
    return matmul_nt(picked, coupling[0]), energy


def third_kernel(counts, corner_map, coupling, inverse, got, local_ref, *refs):
    image_ref, gathered_ref, scalar_ref = refs[:3]
    sends, scratch = refs[3:9], refs[9]
    live = live_of(counts)
    gathered, (resid_dot, local_curve, _, _) = coarse_sums(got, scratch)
    coarse_terms, energy = coarse_solve(inverse, gathered, corner_map, coupling)
    image = live * (local_ref[...] + coarse_terms)
    step_size = resid_dot / (local_curve + energy)
    image_ref[...] = image
    gathered_ref[...] = gathered
    scalar_ref[...] = jnp.concatenate(
        [resid_dot, local_curve, step_size, jnp.zeros((5, LOADS), F32)], axis=0
    )
    store_sends(sends, split_faces(image))


def fourth_kernel(counts, pairing, dirichlet, resid, weight_ref, image_ref, scalar_ref, *refs):
    recvs, (resid_out, terms, dots), sends = refs[:6], refs[6:9], refs[9:]
    live = live_of(counts)
    step_size = column(scalar_ref[2:3, :])
    residual = resid[...] - step_size * (live * (image_ref[...] + partner(recvs, pairing)))
    resid_out[...] = residual
    applied = precondition(weight_ref[0:1, :], residual, dirichlet)
    terms[...] = applied
    dots[...] = load_sums(residual, applied)
    store_sends(sends, split_faces(applied))


def fifth_kernel(counts, pairing, corner_map, schur, coupling, terms, dots, local_ref, *refs):
    recvs, (precond_ref, out) = refs[:6], refs[6:]
    live = live_of(counts)
    precond = live * (terms[...] + partner(recvs, pairing))
    precond_ref[...] = precond
    high = precond.astype(BF16)
    low = (precond - high.astype(F32)).astype(BF16)
    local_terms = live * matmul(high, schur[0])
    both = matmul(jnp.concatenate([high, low], axis=0), coupling[0])
    corner_terms = live * (both[:LOADS] + both[LOADS:])
    square = load_sums(precond, local_terms)
    cross = load_sums(precond, local_ref[...])
    scalars = (dots[0:1], square[0:1], cross[0:1])
    send_message(out, corner_message(corner_map, corner_terms, scalars))


def sixth_kernel(
    counts, corner_map, schur, coupling, inverse, got, gathered_ref, scalar_ref, z_ref, precond_ref, *refs
):
    solution_ref, image_ref, step_ref = refs[:3]
    sends, scratch = refs[3:9], refs[9]
    live = live_of(counts)
    gathered, (new_dot, square, cross, _) = coarse_sums(got, scratch)
    beta = new_dot / scalar_ref[0:1, :]
    gathered = gathered + beta * gathered_ref[...]
    coarse_terms, energy = coarse_solve(inverse, gathered, corner_map, coupling)
    local_curve = square + 2.0 * beta * cross + beta * beta * scalar_ref[1:2, :]
    step_size = new_dot / (local_curve + energy)
    first = z_ref[...]
    direction = precond_ref[...] + column(beta) * first
    local_terms = matmul(direction.astype(BF16), schur[0])
    image = live * (local_terms + coarse_terms)
    image_ref[...] = image
    store_sends(sends, split_faces(image))
    step_ref[...] = jnp.broadcast_to(step_size, (8, LOADS))
    solution_ref[0] = column(scalar_ref[2:3, :]) * first + column(step_size) * direction


def seventh_kernel(counts, pairing, resid, image_ref, step_ref, *refs):
    recvs, (out,) = refs[:6], refs[6:]
    live = live_of(counts)
    image = live * (image_ref[...] + partner(recvs, pairing))
    out[0] = resid[...] - column(step_ref[0:1, :]) * image


def call(kernel, shapes, *operands, scratch=()):
    specs = [SM if operand.shape == (1,) else VM for operand in operands]
    return pl.pallas_call(
        kernel,
        out_shape=[jax.ShapeDtypeStruct(shape, F32) for shape in shapes],
        in_specs=specs,
        out_specs=[VM] * len(shapes),
        scratch_shapes=list(scratch),
        compiler_params=pltpu.CompilerParams(vmem_limit_bytes=32 * 1024 * 1024),
    )(*operands)


def matched(count, start):
    pairs = []
    for low in range(start, count, 2):
        high = (low + 1) % count
        pairs += [(low, high), (high, low)]
    return pairs


def exchange(sends):
    return [
        lax.ppermute(value, AXES[k // 2], matched(SIZES[k // 2], k % 2))
        for k, value in enumerate(sends)
    ]


def spread(message, axes):
    return lax.all_to_all(message, axes, 0, 0)


def local(loads, schur, dirichlet, coupling, coarse_inverse, pairing, corner_map, counts):
    vector = (LOADS, MULT)
    faces = [(LOADS, FACE)] * 6
    small = (8, LOADS)
    solver_scratch = [pltpu.VMEM((COARSE, LOADS), F32)]

    sends = call(prepare_kernel, [(LOADS + 8, FACE)] * 6, counts, loads)
    resid, weight, terms, dots, *sends = call(
        first_kernel, [vector, (8, MULT), vector, small] + faces,
        counts, loads, pairing, dirichlet, *exchange(sends),
    )
    first, local_terms, message = call(
        second_kernel, [vector, vector, (SIDE, 8, FACE)],
        counts, pairing, corner_map, schur, coupling, terms, dots, *exchange(sends),
    )
    (message,) = call(plane_kernel, [(SIZES[0], 72, FACE)], spread(message, ("gy", "gz")))
    image, gathered, scalars, *sends = call(
        third_kernel, [vector, (COARSE, LOADS), small] + faces,
        counts, corner_map, coupling, coarse_inverse, spread(message, "region"), local_terms,
        scratch=solver_scratch,
    )
    resid, terms, dots, *sends = call(
        fourth_kernel, [vector, vector, small] + faces,
        counts, pairing, dirichlet, resid, weight, image, scalars, *exchange(sends),
    )
    precond, message = call(
        fifth_kernel, [vector, (SIDE, 8, FACE)],
        counts, pairing, corner_map, schur, coupling, terms, dots, local_terms, *exchange(sends),
    )
    (message,) = call(plane_kernel, [(SIZES[0], 72, FACE)], spread(message, ("gy", "gz")))
    solution_out, image, step, *sends = call(
        sixth_kernel, [(1,) + vector, vector, small] + faces,
        counts, corner_map, schur, coupling, coarse_inverse, spread(message, "region"),
        gathered, scalars, first, precond, scratch=solver_scratch,
    )
    (residual_out,) = call(
        seventh_kernel, [(1,) + vector],
        counts, pairing, resid, image, step, *exchange(sends),
    )
    return solution_out, residual_out


def solution(mesh):
    block = P(AXES, None, None)
    in_specs = (block, block, block, block, P(), block, P(AXES, None), P(AXES))
    return jax.shard_map(
        local, mesh=mesh, in_specs=in_specs, out_specs=(block, block), check_vma=False
    )
```

```python
import jax
import jax.numpy as jnp
from jax import lax
from jax.experimental import pallas as pl
from jax.experimental.pallas import tpu as pltpu
from jax.sharding import PartitionSpec as P

AXES = ("region", "gy", "gz")
SIZES = (8, 8, 4)
F32 = jnp.float32
BF16 = jnp.bfloat16
LOADS = 32
FACE = 128
MULT = 768
COARSE = 512
SIDE = 32
HIGHEST = lax.Precision.HIGHEST
VM = pl.BlockSpec(memory_space=pltpu.VMEM)
SMEM = pl.BlockSpec(memory_space=pltpu.SMEM)


def matmul(left, right):
    return jnp.dot(left, right, preferred_element_type=F32)


def matmul_nt(left, right, precision=None):
    return lax.dot_general(
        left, right, (((1,), (1,)), ((), ())), precision=precision, preferred_element_type=F32
    )


def coords():
    return [lax.axis_index(axis) for axis in AXES]


def store_sends(sends, faces):
    for e, place in enumerate(coords()):
        odd = place % 2 == 1
        sends[2 * e][...] = jnp.where(odd, faces[2 * e], faces[2 * e + 1])
        sends[2 * e + 1][...] = jnp.where(odd, faces[2 * e + 1], faces[2 * e])


def received_faces(recvs, rows):
    out = []
    for e, place in enumerate(coords()):
        odd = place % 2 == 1
        first, second = recvs[2 * e][rows, :], recvs[2 * e + 1][rows, :]
        lower = jnp.where(odd, first, second)
        upper = jnp.where(odd, second, first)
        out.append(jnp.where(place > 0, lower, 0.0))
        out.append(jnp.where(place < SIZES[e] - 1, upper, 0.0))
    return out


def partner(recvs, pairing, rows=slice(0, LOADS)):
    faces = received_faces(recvs, rows)
    parts = []
    for f in range(6):
        index = jnp.broadcast_to(pairing[f], faces[f].shape)
        parts.append(jnp.take_along_axis(faces[f], index, axis=1))
    return jnp.concatenate(parts, axis=1)


def split_faces(value):
    return [value[:, f * FACE : (f + 1) * FACE] for f in range(6)]


def load_sums(left, right):
    return matmul_nt(jnp.ones((8, MULT), F32), left * right, HIGHEST)


def column(row):
    r = lax.broadcasted_iota(jnp.int32, (LOADS, LOADS), 0)
    c = lax.broadcasted_iota(jnp.int32, (LOADS, LOADS), 1)
    return jnp.sum(jnp.where(r == c, row, 0.0), axis=1, keepdims=True)


def living_kernel(counts, live_ref):
    live_ref[...] = jnp.full((8, FACE), (counts[0] > 0).astype(F32), F32)


def prepare_kernel(live_ref, loads, *sends):
    mark = live_ref[...]
    value = loads[0] * mark[0:1, 0:1]
    faces = [jnp.concatenate([face, mark], axis=0) for face in split_faces(value)]
    store_sends(sends, faces)


def copy_kernel(source, out):
    out[...] = source[...]


def precondition(weight, residual, dirichlet):
    scaled = (weight * residual).astype(BF16)
    return weight * matmul(scaled, dirichlet[0])


def first_kernel(live_ref, loads, pairing, dirichlet, *refs):
    recvs, (resid, weight_ref, terms, dots), sends = refs[:6], refs[6:10], refs[10:]
    live = live_ref[0:1, 0:1]
    residual = live * (loads[0] * live + partner(recvs, pairing))
    multiplicity = live * (live + partner(recvs, pairing, slice(LOADS, LOADS + 8)))
    weight = live / jnp.maximum(multiplicity, 1.0)
    weight_ref[...] = weight
    resid[...] = residual
    applied = precondition(weight[0:1], residual, dirichlet)
    terms[...] = applied
    dots[...] = load_sums(residual, applied)
    store_sends(sends, split_faces(applied))


def corner_message(corner_map, corner_terms, scalars):
    place = coords()
    devices = []
    for step in ((0, 0, 0), (1, 0, 0), (-1, 0, 0), None, (0, 1, 0), (0, -1, 0), (0, 0, 1), (0, 0, -1)):
        if step is None:
            devices.append(None)
            continue
        a, b, c = [(p + s + n) % n for p, s, n in zip(place, step, SIZES)]
        devices.append((a * SIZES[1] + b) * SIZES[2] + c)
    row = lax.broadcasted_iota(jnp.int32, (16, FACE), 0)
    target = jnp.full((16, FACE), -1, jnp.int32)
    for index, device in enumerate(devices):
        for which in range(2):
            at = which * 8 + (index % 2) * 4 + index // 2
            if device is not None:
                target = jnp.where(row == at, device * 2 + which, target)
    chosen = (target == corner_map[0:1, :]).astype(F32)
    sums = matmul_nt(chosen, corner_terms, HIGHEST)
    body = jnp.concatenate([sums[0:4], sums[8:12], sums[4:8], sums[12:16]], axis=1)
    zero = jnp.zeros((1, LOADS), F32)
    tail = jnp.concatenate(list(scalars) + [zero] * (4 - len(scalars)), axis=1)
    return jnp.concatenate([body, jnp.broadcast_to(tail, (4, FACE))], axis=0)


def send_message(out, message):
    for peer in range(out.shape[0]):
        out[peer] = message


def second_kernel(live_ref, pairing, corner_map, schur, coupling, terms, dots, *refs):
    recvs, (z_ref, local_ref, out) = refs[:6], refs[6:]
    live = live_ref[0:1, 0:1]
    direction = live * (terms[...] + partner(recvs, pairing))
    dir_bf = direction.astype(BF16)
    local_terms = live * matmul(dir_bf, schur[0])
    corner_terms = live * matmul(dir_bf, coupling[0])
    z_ref[...] = direction
    local_ref[...] = local_terms
    curve = load_sums(direction, local_terms)
    send_message(out, corner_message(corner_map, corner_terms, (dots[0:1], curve[0:1])))


def plane_kernel(got, out):
    rows = lax.broadcasted_iota(jnp.int32, (SIDE, FACE), 0) % SIZES[2]
    lane = lax.broadcasted_iota(jnp.int32, (SIDE, FACE), 1)
    along_b = got[:, 2, :]
    along_c = got[:, 3, :]
    b_up = pltpu.roll(along_b, SIZES[2], 0)
    b_down = pltpu.roll(pltpu.roll(along_b, SIDE - SIZES[2], 0), 64, 1)
    c_up = jnp.where(rows == 0, pltpu.roll(along_c, SIDE - 3, 0), pltpu.roll(along_c, 1, 0))
    c_down = jnp.where(rows == 3, pltpu.roll(along_c, 3, 0), pltpu.roll(along_c, SIDE - 1, 0))
    c_down = pltpu.roll(c_down, 64, 1)
    own = got[:, 0, :] + jnp.where(lane < 64, (b_up + b_down) + (c_up + c_down), 0.0)
    down = got[:, 1, :]
    scalars = jnp.broadcast_to(jnp.sum(got[:, 4, :], axis=0, keepdims=True), (8, FACE))
    half = SIDE // 2
    down = jnp.where(lane[:half] < 64, down[:half], pltpu.roll(down[half:], 64, 1))
    for peer in range(SIZES[0]):
        out[peer, 0:32, :] = own
        out[peer, 32:48, :] = down
        out[peer, 48:56, :] = scalars


def coarse_sums(got, scratch):
    pieces = []
    for a in range(SIZES[0]):
        below, above = (a + 7) % 8, (a + 1) % 8
        down = got[above, 32:48, :]
        down = jnp.concatenate([down, pltpu.roll(down, 64, 1)], axis=0)
        pieces.append(got[a, 0:32, :] + pltpu.roll(got[below, 0:32, :], 64, 1) + down)
    whole = jnp.concatenate(pieces, axis=0)
    scratch[pl.Slice(0, COARSE // 2, 2), :] = whole[:, 0:32]
    scratch[pl.Slice(1, COARSE // 2, 2), :] = whole[:, 32:64]
    scalars = got[0, 48:56, :]
    for a in range(1, SIZES[0]):
        scalars = scalars + got[a, 48:56, :]
    return scratch[...], [scalars[0:1, i * 32 : i * 32 + 32] for i in range(4)]


def halves(value):
    high = value.astype(BF16)
    return high, (value - high.astype(F32)).astype(BF16)


def coarse_solve(inverse, gathered, corner_map, coupling):
    mat_high, mat_low = halves(inverse[...])
    vec_high, vec_low = halves(gathered)
    both = matmul(mat_high, jnp.concatenate([vec_high, vec_low], axis=1))
    solved = both[:, :LOADS] + (both[:, LOADS:] + matmul(mat_low, vec_high))
    solved = solved.astype(BF16)
    row = lax.broadcasted_iota(jnp.int32, (COARSE, FACE), 0)
    chosen = (row == corner_map[0:1, :]).astype(F32).astype(BF16)
    picked = lax.dot_general(
        solved, chosen, (((0,), (0,)), ((), ())), preferred_element_type=F32
    ).astype(BF16)
    energy = jnp.sum(solved.astype(F32) * gathered, axis=0, keepdims=True)
    return matmul_nt(picked, coupling[0]), energy


def third_kernel(live_ref, corner_map, coupling, inverse, got, local_ref, *refs):
    image_ref, gathered_ref, scalar_ref = refs[:3]
    sends, scratch = refs[3:9], refs[9]
    live = live_ref[0:1, 0:1]
    gathered, (resid_dot, local_curve, _, _) = coarse_sums(got, scratch)
    coarse_terms, energy = coarse_solve(inverse, gathered, corner_map, coupling)
    image = live * (local_ref[...] + coarse_terms)
    step_size = resid_dot / (local_curve + energy)
    image_ref[...] = image
    gathered_ref[...] = gathered
    scalar_ref[...] = jnp.concatenate(
        [resid_dot, local_curve, step_size, jnp.zeros((5, LOADS), F32)], axis=0
    )
    store_sends(sends, split_faces(image))


def fourth_kernel(live_ref, pairing, dirichlet, resid, weight_ref, image_ref, scalar_ref, *refs):
    recvs, (resid_out, terms, dots), sends = refs[:6], refs[6:9], refs[9:]
    live = live_ref[0:1, 0:1]
    step_size = column(scalar_ref[2:3, :])
    residual = resid[...] - step_size * (live * (image_ref[...] + partner(recvs, pairing)))
    resid_out[...] = residual
    applied = precondition(weight_ref[0:1, :], residual, dirichlet)
    terms[...] = applied
    dots[...] = load_sums(residual, applied)
    store_sends(sends, split_faces(applied))


def fifth_kernel(live_ref, pairing, corner_map, schur, coupling, terms, dots, local_ref, *refs):
    recvs, (precond_ref, out) = refs[:6], refs[6:]
    live = live_ref[0:1, 0:1]
    precond = live * (terms[...] + partner(recvs, pairing))
    precond_ref[...] = precond
    high, low = halves(precond)
    local_terms = live * matmul(high, schur[0])
    both = matmul(jnp.concatenate([high, low], axis=0), coupling[0])
    corner_terms = live * (both[:LOADS] + both[LOADS:])
    square = load_sums(precond, local_terms)
    cross = load_sums(precond, local_ref[...])
    scalars = (dots[0:1], square[0:1], cross[0:1])
    send_message(out, corner_message(corner_map, corner_terms, scalars))


def sixth_kernel(
    live_ref, corner_map, schur, coupling, inverse, got, gathered_ref, scalar_ref, z_ref, precond_ref, *refs
):
    solution_ref, image_ref, step_ref = refs[:3]
    sends, scratch = refs[3:9], refs[9]
    live = live_ref[0:1, 0:1]
    gathered, (new_dot, square, cross, _) = coarse_sums(got, scratch)
    beta = new_dot / scalar_ref[0:1, :]
    gathered = gathered + beta * gathered_ref[...]
    coarse_terms, energy = coarse_solve(inverse, gathered, corner_map, coupling)
    local_curve = square + 2.0 * beta * cross + beta * beta * scalar_ref[1:2, :]
    step_size = new_dot / (local_curve + energy)
    first = z_ref[...]
    direction = precond_ref[...] + column(beta) * first
    local_terms = matmul(direction.astype(BF16), schur[0])
    image = live * (local_terms + coarse_terms)
    image_ref[...] = image
    store_sends(sends, split_faces(image))
    step_ref[...] = jnp.broadcast_to(step_size, (8, LOADS))
    solution_ref[0] = column(scalar_ref[2:3, :]) * first + column(step_size) * direction


def seventh_kernel(live_ref, pairing, resid, image_ref, step_ref, *refs):
    recvs, (out,) = refs[:6], refs[6:]
    live = live_ref[0:1, 0:1]
    image = live * (image_ref[...] + partner(recvs, pairing))
    out[0] = resid[...] - column(step_ref[0:1, :]) * image


def call(kernel, shapes, *operands, scratch=(), cost=None, spec=VM):
    return pl.pallas_call(
        kernel,
        out_shape=[
            shape if hasattr(shape, "dtype") else jax.ShapeDtypeStruct(shape, F32)
            for shape in shapes
        ],
        in_specs=[spec] * len(operands),
        out_specs=[VM] * len(shapes),
        scratch_shapes=list(scratch),
        cost_estimate=cost,
        compiler_params=pltpu.CompilerParams(vmem_limit_bytes=32 << 20),
    )(*operands)


def matched(count, start):
    pairs = []
    for low in range(start, count, 2):
        high = (low + 1) % count
        pairs += [(low, high), (high, low)]
    return pairs


def exchange(sends):
    return [
        lax.ppermute(value, AXES[k // 2], matched(SIZES[k // 2], k % 2))
        for k, value in enumerate(sends)
    ]


def spread(message, axes):
    return lax.all_to_all(message, axes, 0, 0)


def local(loads, schur, dirichlet, coupling, coarse_inverse, pairing, corner_map, counts):
    vector = (LOADS, MULT)
    faces = [(LOADS, FACE)] * 6
    small = (8, LOADS)
    solver_scratch = [pltpu.VMEM((COARSE, LOADS), F32)]

    pairing = pairing.reshape(6, 1, FACE)
    cost = pl.CostEstimate(flops=0, bytes_accessed=4 << 20, transcendentals=0)
    (live,) = call(living_kernel, [(8, FACE)], counts, spec=SMEM, cost=cost)
    sends = call(prepare_kernel, [(LOADS + 8, FACE)] * 6, live, loads)
    (dirichlet,) = call(copy_kernel, [jax.ShapeDtypeStruct(dirichlet.shape, BF16)], dirichlet)
    inverse = coarse_inverse
    resid, weight, terms, dots, *sends = call(
        first_kernel, [vector, (8, MULT), vector, small] + faces,
        live, loads, pairing, dirichlet, *exchange(sends),
    )
    first, local_terms, message = call(
        second_kernel, [vector, vector, (SIDE, 8, FACE)],
        live, pairing, corner_map, schur, coupling, terms, dots, *exchange(sends),
    )
    (message,) = call(plane_kernel, [(SIZES[0], 56, FACE)], spread(message, ("gy", "gz")))
    image, gathered, scalars, *sends = call(
        third_kernel, [vector, (COARSE, LOADS), small] + faces,
        live, corner_map, coupling, inverse, spread(message, "region"), local_terms,
        scratch=solver_scratch,
    )
    resid, terms, dots, *sends = call(
        fourth_kernel, [vector, vector, small] + faces,
        live, pairing, dirichlet, resid, weight, image, scalars, *exchange(sends),
    )
    precond, message = call(
        fifth_kernel, [vector, (SIDE, 8, FACE)],
        live, pairing, corner_map, schur, coupling, terms, dots, local_terms, *exchange(sends),
    )
    (message,) = call(plane_kernel, [(SIZES[0], 56, FACE)], spread(message, ("gy", "gz")))
    solution_out, image, step, *sends = call(
        sixth_kernel, [(1,) + vector, vector, small] + faces,
        live, corner_map, schur, coupling, inverse, spread(message, "region"),
        gathered, scalars, first, precond, scratch=solver_scratch,
    )
    (residual_out,) = call(
        seventh_kernel, [(1,) + vector],
        live, pairing, resid, image, step, *exchange(sends),
    )
    return solution_out, residual_out


def solution(mesh):
    block = P(AXES, None, None)
    in_specs = (block, block, block, block, P(), block, P(AXES, None), P(AXES))
    return jax.shard_map(
        local, mesh=mesh, in_specs=in_specs, out_specs=(block, block), check_vma=False
    )
```

```python
import jax
import jax.numpy as jnp
from jax import lax
from jax.experimental import pallas as pl
from jax.experimental.pallas import tpu as pltpu
from jax.sharding import PartitionSpec as P

AXES = ("region", "gy", "gz")
SIZES = (8, 8, 4)
F32 = jnp.float32
BF16 = jnp.bfloat16
LOADS = 32
FACE = 128
MULT = 768
COARSE = 512
SIDE = 32
HALF = 16
DEVICES = 256
HIGHEST = lax.Precision.HIGHEST
VM = pl.BlockSpec(memory_space=pltpu.VMEM)
SMEM = pl.BlockSpec(memory_space=pltpu.SMEM)


def matmul(left, right):
    return jnp.dot(left, right, preferred_element_type=F32)


def matmul_nt(left, right, precision=None):
    return lax.dot_general(
        left, right, (((1,), (1,)), ((), ())), precision=precision, preferred_element_type=F32
    )


def coords():
    return [lax.axis_index(axis) for axis in AXES]


def store_sends(sends, faces):
    for e, place in enumerate(coords()):
        odd = place % 2 == 1
        sends[2 * e][...] = jnp.where(odd, faces[2 * e], faces[2 * e + 1])
        sends[2 * e + 1][...] = jnp.where(odd, faces[2 * e + 1], faces[2 * e])


def received_faces(recvs, rows):
    out = []
    for e, place in enumerate(coords()):
        odd = place % 2 == 1
        first, second = recvs[2 * e][rows, :], recvs[2 * e + 1][rows, :]
        lower = jnp.where(odd, first, second)
        upper = jnp.where(odd, second, first)
        out.append(jnp.where(place > 0, lower, 0.0))
        out.append(jnp.where(place < SIZES[e] - 1, upper, 0.0))
    return out


def partner(recvs, pairing, rows=slice(0, LOADS)):
    faces = received_faces(recvs, rows)
    parts = []
    for f in range(6):
        index = jnp.broadcast_to(pairing[f], faces[f].shape)
        parts.append(jnp.take_along_axis(faces[f], index, axis=1))
    return jnp.concatenate(parts, axis=1)


def split_faces(value):
    return [value[:, f * FACE : (f + 1) * FACE] for f in range(6)]


def load_sums(left, right):
    return matmul_nt(jnp.ones((8, MULT), F32), left * right, HIGHEST)


def column(row):
    r = lax.broadcasted_iota(jnp.int32, (LOADS, LOADS), 0)
    c = lax.broadcasted_iota(jnp.int32, (LOADS, LOADS), 1)
    return jnp.sum(jnp.where(r == c, row, 0.0), axis=1, keepdims=True)


def living_kernel(counts, live_ref):
    live_ref[...] = jnp.full((8, FACE), (counts[0] > 0).astype(F32), F32)


def prepare_kernel(live_ref, loads, *sends):
    mark = live_ref[...]
    value = loads[0] * mark[0:1, 0:1]
    faces = [jnp.concatenate([face, mark], axis=0) for face in split_faces(value)]
    store_sends(sends, faces)


def copy_kernel(source, out):
    out[...] = source[...]


def precondition(weight, residual, dirichlet):
    scaled = (weight * residual).astype(BF16)
    return weight * matmul(scaled, dirichlet[0])


def first_kernel(live_ref, loads, pairing, dirichlet, *refs):
    recvs, (resid, weight_ref, terms, dots), sends = refs[:6], refs[6:10], refs[10:]
    live = live_ref[0:1, 0:1]
    residual = live * (loads[0] * live + partner(recvs, pairing))
    multiplicity = live * (live + partner(recvs, pairing, slice(LOADS, LOADS + 8)))
    weight = live / jnp.maximum(multiplicity, 1.0)
    weight_ref[...] = weight
    resid[...] = residual
    applied = precondition(weight[0:1], residual, dirichlet)
    terms[...] = applied
    dots[...] = load_sums(residual, applied)
    store_sends(sends, split_faces(applied))


def corner_message(corner_map, corner_terms, scalars):
    place = coords()
    steps = ((0, 0, 0), (0, 1, 0), (1, 0, 0), (0, -1, 0), (-1, 0, 0), (0, 0, 1), None, (0, 0, -1))
    row = lax.broadcasted_iota(jnp.int32, (16, FACE), 0)
    target = jnp.full((16, FACE), -1, jnp.int32)
    for index, step in enumerate(steps):
        if step is not None:
            a, b, c = [(p + s + n) % n for p, s, n in zip(place, step, SIZES)]
            owned = 2 * ((a * SIZES[1] + b) * SIZES[2] + c)
            target = jnp.where(row == index, owned, target)
            target = jnp.where(row == index + 8, owned + 1, target)
    chosen = (target == corner_map[0:1, :]).astype(F32)
    sums = matmul_nt(chosen, corner_terms, HIGHEST)
    line = lax.broadcasted_iota(jnp.int32, (8, LOADS), 0)
    pair = [
        jnp.where(line == 6, scalar, sums[8 * i : 8 * i + 8]) for i, scalar in enumerate(scalars)
    ]
    messages = []
    for k in range(2):
        part = jnp.concatenate([value[:, k * HALF : (k + 1) * HALF] for value in pair], axis=1)
        messages.append(jnp.concatenate([part[2 * i : 2 * i + 2] for i in range(4)], axis=1))
    return messages


def send_message(out, messages):
    for a in range(SIZES[0]):
        block = jnp.broadcast_to(messages[a % 2][None], (SIDE, 2, FACE))
        out[a * SIDE : (a + 1) * SIDE] = block


def second_kernel(live_ref, pairing, corner_map, schur, coupling, terms, dots, *refs):
    recvs, (z_ref, local_ref, out) = refs[:6], refs[6:]
    live = live_ref[0:1, 0:1]
    direction = live * (terms[...] + partner(recvs, pairing))
    dir_bf = direction.astype(BF16)
    local_terms = live * matmul(dir_bf, schur[0])
    corner_terms = live * matmul(dir_bf, coupling[0])
    z_ref[...] = direction
    local_ref[...] = local_terms
    curve = load_sums(direction, local_terms)
    send_message(out, corner_message(corner_map, corner_terms, (dots[0:1], curve[0:1])))


def combine_kernel(got, out):
    third = lax.broadcasted_iota(jnp.int32, (SIDE, FACE), 0) % SIZES[2]
    total = jnp.zeros((8, FACE), F32)
    for a in range(SIZES[0]):
        def plane(index, line):
            first = (index % SIZES[0]) * SIDE
            return got[first : first + SIDE, line, :]

        here, side = plane(a, 0), plane(a, 1)
        b_up = pltpu.roll(side, SIZES[2], 0)
        b_down = pltpu.roll(side, SIDE - SIZES[2], 0)
        c_up = jnp.where(third == 0, pltpu.roll(side, SIDE - 3, 0), pltpu.roll(side, 1, 0))
        c_down = jnp.where(third == 3, pltpu.roll(side, 3, 0), pltpu.roll(side, SIDE - 1, 0))
        near = here + b_up
        near = near + pltpu.roll(plane(a - 1, 0) + b_down, 96, 1)
        near = near + pltpu.roll(plane(a + 1, 0) + c_up, 64, 1)
        near = near + pltpu.roll(c_down, 32, 1)
        out[a * SIDE : (a + 1) * SIDE, :] = near
        total = total + (here[0:8] + here[8:16]) + (here[16:24] + here[24:32])
    out[DEVICES : DEVICES + 8, :] = jnp.broadcast_to(
        jnp.sum(total, axis=0, keepdims=True), (8, FACE)
    )


def coarse_sums(mine, other, scratch):
    odd = coords()[0] % 2 == 1

    def pieces(rows):
        low = jnp.where(odd, other[rows, :], mine[rows, :])
        high = jnp.where(odd, mine[rows, :], other[rows, :])
        return low, high

    def joined(low, high, start):
        at = pltpu.roll(low, (FACE - start) % FACE, 1) if start else low
        to = pltpu.roll(high, (FACE - start + HALF) % FACE, 1)
        lane = lax.broadcasted_iota(jnp.int32, low.shape, 1)
        return jnp.where(lane < HALF, at, to)[:, 0:LOADS]

    low, high = pieces(slice(0, DEVICES))
    scratch[pl.Slice(0, DEVICES, 2), :] = joined(low, high, 0)
    scratch[pl.Slice(1, DEVICES, 2), :] = joined(low, high, HALF)
    low, high = pieces(slice(DEVICES, DEVICES + 8))
    scalars = [joined(low, high, 96 + i * HALF)[0:1] for i in range(2)]
    return scratch[...], scalars


def halves(value):
    high = value.astype(BF16)
    return high, (value - high.astype(F32)).astype(BF16)


def coarse_solve(inverse, gathered, corner_map, coupling):
    mat_high, mat_low = halves(inverse[...])
    vec_high, vec_low = halves(gathered)
    both = matmul(mat_high, jnp.concatenate([vec_high, vec_low], axis=1))
    solved = both[:, :LOADS] + (both[:, LOADS:] + matmul(mat_low, vec_high))
    solved = solved.astype(BF16)
    row = lax.broadcasted_iota(jnp.int32, (COARSE, FACE), 0)
    chosen = (row == corner_map[0:1, :]).astype(F32).astype(BF16)
    picked = lax.dot_general(
        solved, chosen, (((0,), (0,)), ((), ())), preferred_element_type=F32
    ).astype(BF16)
    return matmul_nt(picked, coupling[0]), solved.astype(F32)


def coarse_dot(solved, gathered):
    return jnp.sum(solved * gathered, axis=0, keepdims=True)


def third_kernel(live_ref, corner_map, coupling, inverse, mine, other, local_ref, *refs):
    image_ref, gathered_ref, solved_ref, scalar_ref = refs[:4]
    sends, scratch = refs[4:10], refs[10]
    live = live_ref[0:1, 0:1]
    gathered, (resid_dot, local_curve) = coarse_sums(mine, other, scratch)
    coarse_terms, solved = coarse_solve(inverse, gathered, corner_map, coupling)
    image = live * (local_ref[...] + coarse_terms)
    curvature = local_curve + coarse_dot(solved, gathered)
    step_size = resid_dot / curvature
    image_ref[...] = image
    gathered_ref[...] = gathered
    solved_ref[...] = solved
    scalar_ref[...] = jnp.concatenate(
        [resid_dot, local_curve, step_size, curvature, jnp.zeros((4, LOADS), F32)], axis=0
    )
    store_sends(sends, split_faces(image))


def fourth_kernel(live_ref, pairing, dirichlet, resid, weight_ref, image_ref, scalar_ref, *refs):
    recvs, (resid_out, terms, dots), sends = refs[:6], refs[6:9], refs[9:]
    live = live_ref[0:1, 0:1]
    step_size = column(scalar_ref[2:3, :])
    residual = resid[...] - step_size * (live * (image_ref[...] + partner(recvs, pairing)))
    resid_out[...] = residual
    applied = precondition(weight_ref[0:1, :], residual, dirichlet)
    terms[...] = applied
    dots[...] = load_sums(residual, applied)
    store_sends(sends, split_faces(applied))


def fifth_kernel(live_ref, pairing, corner_map, schur, coupling, terms, dots, *refs):
    recvs, (precond_ref, out) = refs[:6], refs[6:]
    live = live_ref[0:1, 0:1]
    precond = live * (terms[...] + partner(recvs, pairing))
    precond_ref[...] = precond
    high, low = halves(precond)
    local_terms = live * matmul(high, schur[0])
    both = matmul(jnp.concatenate([high, low], axis=0), coupling[0])
    corner_terms = live * (both[:LOADS] + both[LOADS:])
    square = load_sums(precond, local_terms)
    send_message(out, corner_message(corner_map, corner_terms, (dots[0:1], square[0:1])))


def sixth_kernel(
    live_ref, corner_map, schur, coupling, inverse, mine, other, gathered_ref, solved_ref,
    scalar_ref, z_ref, precond_ref, *refs
):
    solution_ref, image_ref, step_ref = refs[:3]
    sends, scratch = refs[3:9], refs[9]
    live = live_ref[0:1, 0:1]
    gathered, (new_dot, square) = coarse_sums(mine, other, scratch)
    beta = new_dot / scalar_ref[0:1, :]
    cross = -beta * scalar_ref[3:4, :] - coarse_dot(solved_ref[...], gathered)
    gathered = gathered + beta * gathered_ref[...]
    coarse_terms, solved = coarse_solve(inverse, gathered, corner_map, coupling)
    local_curve = square + beta * (2.0 * cross + beta * scalar_ref[1:2, :])
    step_size = new_dot / (local_curve + coarse_dot(solved, gathered))
    first = z_ref[...]
    direction = precond_ref[...] + column(beta) * first
    local_terms = matmul(direction.astype(BF16), schur[0])
    image = live * (local_terms + coarse_terms)
    image_ref[...] = image
    store_sends(sends, split_faces(image))
    step_ref[...] = jnp.broadcast_to(step_size, (8, LOADS))
    solution_ref[0] = column(scalar_ref[2:3, :]) * first + column(step_size) * direction


def seventh_kernel(live_ref, pairing, resid, image_ref, step_ref, *refs):
    recvs, (out,) = refs[:6], refs[6:]
    live = live_ref[0:1, 0:1]
    image = live * (image_ref[...] + partner(recvs, pairing))
    out[0] = resid[...] - column(step_ref[0:1, :]) * image


def call(kernel, shapes, *operands, scratch=(), cost=None, spec=VM):
    return pl.pallas_call(
        kernel,
        out_shape=[
            shape if hasattr(shape, "dtype") else jax.ShapeDtypeStruct(shape, F32)
            for shape in shapes
        ],
        in_specs=[spec] * len(operands),
        out_specs=[VM] * len(shapes),
        scratch_shapes=list(scratch),
        cost_estimate=cost,
        compiler_params=pltpu.CompilerParams(vmem_limit_bytes=32 << 20),
    )(*operands)


def matched(count, start):
    pairs = []
    for low in range(start, count, 2):
        high = (low + 1) % count
        pairs += [(low, high), (high, low)]
    return pairs


def exchange(sends):
    return [
        lax.ppermute(value, AXES[k // 2], matched(SIZES[k // 2], k % 2))
        for k, value in enumerate(sends)
    ]


def total_sums(message):
    (mine,) = call(combine_kernel, [(DEVICES + 8, FACE)], lax.all_to_all(message, AXES, 0, 0))
    return mine, lax.ppermute(mine, AXES[0], matched(SIZES[0], 0))


def local(loads, schur, dirichlet, coupling, coarse_inverse, pairing, corner_map, counts):
    vector = (LOADS, MULT)
    faces = [(LOADS, FACE)] * 6
    small = (8, LOADS)
    solver_scratch = [pltpu.VMEM((COARSE, LOADS), F32)]

    pairing = pairing.reshape(6, 1, FACE)
    cost = pl.CostEstimate(flops=0, bytes_accessed=4 << 20, transcendentals=0)
    (live,) = call(living_kernel, [(8, FACE)], counts, spec=SMEM, cost=cost)
    sends = call(prepare_kernel, [(LOADS + 8, FACE)] * 6, live, loads)
    (dirichlet,) = call(copy_kernel, [jax.ShapeDtypeStruct(dirichlet.shape, BF16)], dirichlet)
    inverse = coarse_inverse
    resid, weight, terms, dots, *sends = call(
        first_kernel, [vector, (8, MULT), vector, small] + faces,
        live, loads, pairing, dirichlet, *exchange(sends),
    )
    first, local_terms, message = call(
        second_kernel, [vector, vector, (DEVICES, 2, FACE)],
        live, pairing, corner_map, schur, coupling, terms, dots, *exchange(sends),
    )
    image, gathered, solved, scalars, *sends = call(
        third_kernel, [vector, (COARSE, LOADS), (COARSE, LOADS), small] + faces,
        live, corner_map, coupling, inverse, *total_sums(message), local_terms,
        scratch=solver_scratch,
    )
    resid, terms, dots, *sends = call(
        fourth_kernel, [vector, vector, small] + faces,
        live, pairing, dirichlet, resid, weight, image, scalars, *exchange(sends),
    )
    precond, message = call(
        fifth_kernel, [vector, (DEVICES, 2, FACE)],
        live, pairing, corner_map, schur, coupling, terms, dots, *exchange(sends),
    )
    solution_out, image, step, *sends = call(
        sixth_kernel, [(1,) + vector, vector, small] + faces,
        live, corner_map, schur, coupling, inverse, *total_sums(message),
        gathered, solved, scalars, first, precond, scratch=solver_scratch,
    )
    (residual_out,) = call(
        seventh_kernel, [(1,) + vector],
        live, pairing, resid, image, step, *exchange(sends),
    )
    return solution_out, residual_out


def solution(mesh):
    block = P(AXES, None, None)
    in_specs = (block, block, block, block, P(), block, P(AXES, None), P(AXES))
    return jax.shard_map(
        local, mesh=mesh, in_specs=in_specs, out_specs=(block, block), check_vma=False
    )
```

```python
import jax
import jax.numpy as jnp
from jax import lax
from jax.experimental import pallas as pl
from jax.experimental.pallas import tpu as pltpu
from jax.sharding import PartitionSpec as P

AXES = ("region", "gy", "gz")
SIZES = (8, 8, 4)
F32 = jnp.float32
BF16 = jnp.bfloat16
LOADS = 32
FACE = 128
MULT = 768
COARSE = 512
SIDE = 32
HALF = 16
DEVICES = 256
VM = pl.BlockSpec(memory_space=pltpu.VMEM)
SMEM = pl.BlockSpec(memory_space=pltpu.SMEM)


def matmul(left, right):
    return jnp.dot(left, right, preferred_element_type=F32)


def halves(value):
    high = value.astype(BF16)
    return high, (value - high.astype(F32)).astype(BF16)


def matmul_nt(left, right):
    return lax.dot_general(left, right, (((1,), (1,)), ((), ())), preferred_element_type=F32)


def coords():
    return [lax.axis_index(axis) for axis in AXES]


ORDER = (1, 2, 3, 4, 5, 0)


def store_sends(sends, faces):
    for e, place in enumerate(coords()):
        odd = place % 2 == 1
        first, second = ORDER.index(2 * e), ORDER.index(2 * e + 1)
        sends[first][...] = jnp.where(odd, faces[2 * e], faces[2 * e + 1])
        sends[second][...] = jnp.where(odd, faces[2 * e + 1], faces[2 * e])


def received_faces(recvs, rows):
    out = []
    for e, place in enumerate(coords()):
        odd = place % 2 == 1
        first = recvs[ORDER.index(2 * e)][rows, :]
        second = recvs[ORDER.index(2 * e + 1)][rows, :]
        lower = jnp.where(odd, first, second)
        upper = jnp.where(odd, second, first)
        out.append(jnp.where(place > 0, lower, 0.0))
        out.append(jnp.where(place < SIZES[e] - 1, upper, 0.0))
    return out


def partner(recvs, pairing, rows=slice(0, LOADS)):
    faces = received_faces(recvs, rows)
    parts = []
    for f in range(6):
        index = jnp.broadcast_to(pairing[f], faces[f].shape)
        parts.append(jnp.take_along_axis(faces[f], index, axis=1))
    return jnp.concatenate(parts, axis=1)


def split_faces(value):
    return [value[:, f * FACE : (f + 1) * FACE] for f in range(6)]


def select_nt(table, value):
    rows = value.shape[0]
    high, _ = halves(value)
    middle, low = halves(value - high.astype(F32))
    out = matmul_nt(table, jnp.concatenate([high, middle, low], axis=0))
    return out[:, :rows] + (out[:, rows : 2 * rows] + out[:, 2 * rows :])


def load_sums(left, right):
    return select_nt(jnp.ones((8, MULT), BF16), left * right)


def column(row):
    r = lax.broadcasted_iota(jnp.int32, (LOADS, LOADS), 0)
    c = lax.broadcasted_iota(jnp.int32, (LOADS, LOADS), 1)
    return jnp.sum(jnp.where(r == c, row, 0.0), axis=1, keepdims=True)


def living_kernel(counts, live_ref):
    live_ref[...] = jnp.full((8, FACE), (counts[0] > 0).astype(F32), F32)


def prepare_kernel(live_ref, loads, *sends):
    mark = live_ref[...]
    value = loads[0] * mark[0:1, 0:1]
    faces = [jnp.concatenate([face, mark], axis=0) for face in split_faces(value)]
    store_sends(sends, faces)


def copy_kernel(source, out):
    out[...] = source[...]


def halves_kernel(source, after, out):
    out[0], out[1] = halves(source[...])


def precondition(weight, residual, dirichlet):
    scaled = (weight * residual).astype(BF16)
    return weight * matmul(scaled, dirichlet[0])


def first_kernel(live_ref, loads, pairing, dirichlet, *refs):
    recvs, (resid, weight_ref, terms, dots), sends = refs[:6], refs[6:10], refs[10:]
    live = live_ref[0:1, 0:1]
    residual = live * (loads[0] * live + partner(recvs, pairing))
    multiplicity = live * (live + partner(recvs, pairing, slice(LOADS, LOADS + 8)))
    weight = live / jnp.maximum(multiplicity, 1.0)
    weight_ref[...] = weight
    resid[...] = residual
    applied = precondition(weight[0:1], residual, dirichlet)
    terms[...] = applied
    dots[...] = load_sums(residual, applied)
    store_sends(sends, split_faces(applied))


def corner_message(corner_map, corner_terms, scalars):
    place = coords()
    steps = ((0, 0, 0), (0, 1, 0), (1, 0, 0), (0, -1, 0), (-1, 0, 0), (0, 0, 1), None, (0, 0, -1))
    row = lax.broadcasted_iota(jnp.int32, (16, FACE), 0)
    target = jnp.full((16, FACE), -1, jnp.int32)
    for index, step in enumerate(steps):
        if step is not None:
            a, b, c = [(p + s + n) % n for p, s, n in zip(place, step, SIZES)]
            owned = 2 * ((a * SIZES[1] + b) * SIZES[2] + c)
            target = jnp.where(row == index, owned, target)
            target = jnp.where(row == index + 8, owned + 1, target)
    chosen = (target == corner_map[0:1, :]).astype(F32).astype(BF16)
    sums = select_nt(chosen, corner_terms)
    line = lax.broadcasted_iota(jnp.int32, (8, LOADS), 0)
    pair = [
        jnp.where(line == 6, scalar, sums[8 * i : 8 * i + 8]) for i, scalar in enumerate(scalars)
    ]
    messages = []
    for k in range(2):
        part = jnp.concatenate([value[:, k * HALF : (k + 1) * HALF] for value in pair], axis=1)
        messages.append(jnp.concatenate([part[2 * i : 2 * i + 2] for i in range(4)], axis=1))
    return messages


def send_message(out, messages):
    block = jnp.stack(messages * (SIZES[0] // 2))
    for i in range(SIDE):
        out[i * SIZES[0] : (i + 1) * SIZES[0]] = block


def second_kernel(live_ref, pairing, corner_map, schur, coupling, terms, dots, *refs):
    recvs, (z_ref, local_ref, out) = refs[:6], refs[6:]
    live = live_ref[0:1, 0:1]
    direction = live * (terms[...] + partner(recvs, pairing))
    dir_bf = direction.astype(BF16)
    local_terms = live * matmul(dir_bf, schur[0])
    corner_terms = live * matmul(dir_bf, coupling[0])
    z_ref[...] = direction
    local_ref[...] = local_terms
    curve = load_sums(direction, local_terms)
    send_message(out, corner_message(corner_map, corner_terms, (dots[0:1], curve[0:1])))


BY_COLUMN = ("gy", "gz", "region")


def combine_kernel(got, out):
    total = jnp.zeros((8, FACE), F32)

    def column(b, c, line):
        first = (b % SIZES[1] * SIZES[2] + c % SIZES[2]) * SIZES[0]
        return got[first : first + SIZES[0], line, :]

    for b in range(SIZES[1]):
        for c in range(SIZES[2]):
            here = column(b, c, 0)
            near = here + column(b - 1, c, 1)
            near = near + pltpu.roll(pltpu.roll(here, 1, 0) + column(b + 1, c, 1), 96, 1)
            near = near + pltpu.roll(pltpu.roll(here, 7, 0) + column(b, c - 1, 1), 64, 1)
            near = near + pltpu.roll(column(b, c + 1, 1), 32, 1)
            out[pl.Slice(b * SIZES[2] + c, SIZES[0], SIDE), :] = near
            total = total + here
    out[DEVICES : DEVICES + 8, :] = jnp.broadcast_to(
        jnp.sum(total, axis=0, keepdims=True), (8, FACE)
    )


def coarse_sums(mine, other, scratch):
    odd = coords()[0] % 2 == 1

    def pieces(rows):
        low = jnp.where(odd, other[rows, :], mine[rows, :])
        high = jnp.where(odd, mine[rows, :], other[rows, :])
        return low, high

    def joined(low, high, start):
        at = pltpu.roll(low, (FACE - start) % FACE, 1) if start else low
        to = pltpu.roll(high, (FACE - start + HALF) % FACE, 1)
        lane = lax.broadcasted_iota(jnp.int32, low.shape, 1)
        return jnp.where(lane < HALF, at, to)[:, 0:LOADS]

    low, high = pieces(slice(0, DEVICES))
    scratch[pl.Slice(0, DEVICES, 2), :] = joined(low, high, 0)
    scratch[pl.Slice(1, DEVICES, 2), :] = joined(low, high, HALF)
    low, high = pieces(slice(DEVICES, DEVICES + 8))
    scalars = [joined(low, high, 96 + i * HALF)[0:1] for i in range(2)]
    return scratch[...], scalars


def coarse_solve(inverse, gathered, corner_map, coupling):
    vec_high, vec_low = halves(gathered)
    both = matmul(inverse[0], jnp.concatenate([vec_high, vec_low], axis=1))
    solved = both[:, :LOADS] + (both[:, LOADS:] + matmul(inverse[1], vec_high))
    solved = solved.astype(BF16)
    row = lax.broadcasted_iota(jnp.int32, (COARSE, FACE), 0)
    chosen = (row == corner_map[0:1, :]).astype(F32).astype(BF16)
    picked = lax.dot_general(
        solved, chosen, (((0,), (0,)), ((), ())), preferred_element_type=F32
    ).astype(BF16)
    return matmul_nt(picked, coupling[0]), solved.astype(F32)


def coarse_dot(solved, gathered):
    return jnp.sum(solved * gathered, axis=0, keepdims=True)


def third_kernel(live_ref, corner_map, coupling, inverse, mine, other, local_ref, *refs):
    image_ref, gathered_ref, solved_ref, scalar_ref = refs[:4]
    sends, scratch = refs[4:10], refs[10]
    live = live_ref[0:1, 0:1]
    gathered, (resid_dot, local_curve) = coarse_sums(mine, other, scratch)
    coarse_terms, solved = coarse_solve(inverse, gathered, corner_map, coupling)
    image = live * (local_ref[...] + coarse_terms)
    curvature = local_curve + coarse_dot(solved, gathered)
    step_size = resid_dot / curvature
    image_ref[...] = image
    gathered_ref[...] = gathered
    solved_ref[...] = solved
    scalar_ref[...] = jnp.concatenate(
        [resid_dot, local_curve, step_size, curvature, jnp.zeros((4, LOADS), F32)], axis=0
    )
    store_sends(sends, split_faces(image))


def fourth_kernel(live_ref, pairing, dirichlet, resid, weight_ref, image_ref, scalar_ref, *refs):
    recvs, (resid_out, terms, dots), sends = refs[:6], refs[6:9], refs[9:]
    live = live_ref[0:1, 0:1]
    step_size = column(scalar_ref[2:3, :])
    residual = resid[...] - step_size * (live * (image_ref[...] + partner(recvs, pairing)))
    resid_out[...] = residual
    applied = precondition(weight_ref[0:1, :], residual, dirichlet)
    terms[...] = applied
    dots[...] = load_sums(residual, applied)
    store_sends(sends, split_faces(applied))


def fifth_kernel(live_ref, pairing, corner_map, schur, coupling, terms, dots, *refs):
    recvs, (precond_ref, out) = refs[:6], refs[6:]
    live = live_ref[0:1, 0:1]
    precond = live * (terms[...] + partner(recvs, pairing))
    precond_ref[...] = precond
    high, low = halves(precond)
    local_terms = live * matmul(high, schur[0])
    both = matmul(jnp.concatenate([high, low], axis=0), coupling[0])
    corner_terms = live * (both[:LOADS] + both[LOADS:])
    square = load_sums(precond, local_terms)
    send_message(out, corner_message(corner_map, corner_terms, (dots[0:1], square[0:1])))


def sixth_kernel(
    live_ref, corner_map, schur, coupling, inverse, mine, other, gathered_ref, solved_ref,
    scalar_ref, z_ref, precond_ref, *refs
):
    direction_ref, image_ref, step_ref = refs[:3]
    sends, scratch = refs[3:9], refs[9]
    live = live_ref[0:1, 0:1]
    gathered, (new_dot, square) = coarse_sums(mine, other, scratch)
    beta = new_dot / scalar_ref[0:1, :]
    cross = -beta * scalar_ref[3:4, :] - coarse_dot(solved_ref[...], gathered)
    gathered = gathered + beta * gathered_ref[...]
    coarse_terms, solved = coarse_solve(inverse, gathered, corner_map, coupling)
    local_curve = square + beta * (2.0 * cross + beta * scalar_ref[1:2, :])
    step_size = new_dot / (local_curve + coarse_dot(solved, gathered))
    first = z_ref[...]
    direction = precond_ref[...] + column(beta) * first
    local_terms = matmul(direction.astype(BF16), schur[0])
    image = live * (local_terms + coarse_terms)
    image_ref[...] = image
    store_sends(sends, split_faces(image))
    step_ref[...] = jnp.broadcast_to(step_size, (8, LOADS))
    direction_ref[...] = direction


def solution_kernel(scalar_ref, first, step_ref, direction, out):
    out[0] = column(scalar_ref[2:3, :]) * first[...] + column(step_ref[0:1, :]) * direction[...]


def seventh_kernel(live_ref, pairing, resid, image_ref, step_ref, *refs):
    recvs, (out,) = refs[:6], refs[6:]
    live = live_ref[0:1, 0:1]
    image = live * (image_ref[...] + partner(recvs, pairing))
    out[0] = resid[...] - column(step_ref[0:1, :]) * image


def call(kernel, shapes, *operands, scratch=(), cost=None, spec=VM):
    return pl.pallas_call(
        kernel,
        out_shape=[
            shape if hasattr(shape, "dtype") else jax.ShapeDtypeStruct(shape, F32)
            for shape in shapes
        ],
        in_specs=[spec] * len(operands),
        out_specs=[VM] * len(shapes),
        scratch_shapes=list(scratch),
        cost_estimate=cost,
        compiler_params=pltpu.CompilerParams(vmem_limit_bytes=32 << 20),
    )(*operands)


def matched(count, start):
    pairs = []
    for low in range(start, count, 2):
        high = (low + 1) % count
        pairs += [(low, high), (high, low)]
    return pairs


def exchange(sends):
    return [
        lax.ppermute(value, AXES[k // 2], matched(SIZES[k // 2], k % 2))
        for k, value in zip(ORDER, sends)
    ]


def total_sums(message):
    (mine,) = call(combine_kernel, [(DEVICES + 8, FACE)], lax.all_to_all(message, BY_COLUMN, 0, 0))
    return mine, lax.ppermute(mine, AXES[0], matched(SIZES[0], 0))


def local(loads, schur, dirichlet, coupling, coarse_inverse, pairing, corner_map, counts):
    vector = (LOADS, MULT)
    faces = [(LOADS, FACE)] * 6
    small = (8, LOADS)
    solver_scratch = [pltpu.VMEM((COARSE, LOADS), F32)]

    pairing = pairing.reshape(6, 1, FACE)
    cost = pl.CostEstimate(flops=0, bytes_accessed=4 << 20, transcendentals=0)
    (live,) = call(living_kernel, [(8, FACE)], counts, spec=SMEM, cost=cost)
    sends = call(prepare_kernel, [(LOADS + 8, FACE)] * 6, live, loads)
    (dirichlet,) = call(copy_kernel, [jax.ShapeDtypeStruct(dirichlet.shape, BF16)], dirichlet)
    resid, weight, terms, dots, *sends = call(
        first_kernel, [vector, (8, MULT), vector, small] + faces,
        live, loads, pairing, dirichlet, *exchange(sends),
    )
    (inverse,) = call(
        halves_kernel, [jax.ShapeDtypeStruct((2, COARSE, COARSE), BF16)], coarse_inverse, dots
    )
    first, local_terms, message = call(
        second_kernel, [vector, vector, (DEVICES, 2, FACE)],
        live, pairing, corner_map, schur, coupling, terms, dots, *exchange(sends),
    )
    image, gathered, solved, scalars, *sends = call(
        third_kernel, [vector, (COARSE, LOADS), (COARSE, LOADS), small] + faces,
        live, corner_map, coupling, inverse, *total_sums(message), local_terms,
        scratch=solver_scratch,
    )
    resid, terms, dots, *sends = call(
        fourth_kernel, [vector, vector, small] + faces,
        live, pairing, dirichlet, resid, weight, image, scalars, *exchange(sends),
    )
    precond, message = call(
        fifth_kernel, [vector, (DEVICES, 2, FACE)],
        live, pairing, corner_map, schur, coupling, terms, dots, *exchange(sends),
    )
    direction, image, step, *sends = call(
        sixth_kernel, [vector, vector, small] + faces,
        live, corner_map, schur, coupling, inverse, *total_sums(message),
        gathered, solved, scalars, first, precond, scratch=solver_scratch,
    )
    (solution_out,) = call(solution_kernel, [(1,) + vector], scalars, first, step, direction)
    (residual_out,) = call(
        seventh_kernel, [(1,) + vector],
        live, pairing, resid, image, step, *exchange(sends),
    )
    return solution_out, residual_out


def solution(mesh):
    block = P(AXES, None, None)
    in_specs = (block, block, block, block, P(), block, P(AXES, None), P(AXES))
    return jax.shard_map(
        local, mesh=mesh, in_specs=in_specs, out_specs=(block, block), check_vma=False
    )
```

```python
import jax
import jax.numpy as jnp
from jax import lax
from jax.experimental import pallas as pl
from jax.experimental.pallas import tpu as pltpu
from jax.sharding import PartitionSpec as P

AXES = ("region", "gy", "gz")
SIZES = (8, 8, 4)
F32 = jnp.float32
BF16 = jnp.bfloat16
LOADS = 32
FACE = 128
MULT = 768
COARSE = 512
SIDE = 32
HALF = 16
DEVICES = 256
HIGHEST = lax.Precision.HIGHEST
VM = pl.BlockSpec(memory_space=pltpu.VMEM)
SMEM = pl.BlockSpec(memory_space=pltpu.SMEM)


def matmul(left, right):
    return jnp.dot(left, right, preferred_element_type=F32)


def halves(value):
    high = value.astype(BF16)
    return high, (value - high.astype(F32)).astype(BF16)


def matmul_nt(left, right):
    return lax.dot_general(left, right, (((1,), (1,)), ((), ())), preferred_element_type=F32)


def coords():
    return [lax.axis_index(axis) for axis in AXES]


ORDER = (1, 2, 3, 4, 5, 0)


def store_sends(sends, faces):
    for e, place in enumerate(coords()):
        odd = place % 2 == 1
        first, second = ORDER.index(2 * e), ORDER.index(2 * e + 1)
        sends[first][...] = jnp.where(odd, faces[2 * e], faces[2 * e + 1])
        sends[second][...] = jnp.where(odd, faces[2 * e + 1], faces[2 * e])


def received_faces(recvs, rows):
    out = []
    for e, place in enumerate(coords()):
        odd = place % 2 == 1
        first = recvs[ORDER.index(2 * e)][rows, :]
        second = recvs[ORDER.index(2 * e + 1)][rows, :]
        lower = jnp.where(odd, first, second)
        upper = jnp.where(odd, second, first)
        out.append(jnp.where(place > 0, lower, 0.0))
        out.append(jnp.where(place < SIZES[e] - 1, upper, 0.0))
    return out


def partner(recvs, pairing, rows=slice(0, LOADS)):
    faces = received_faces(recvs, rows)
    parts = []
    for f in range(6):
        index = jnp.broadcast_to(pairing[f], faces[f].shape)
        parts.append(jnp.take_along_axis(faces[f], index, axis=1))
    return jnp.concatenate(parts, axis=1)


def split_faces(value):
    return [value[:, f * FACE : (f + 1) * FACE] for f in range(6)]


def matmul_nt_exact(left, right):
    return lax.dot_general(
        left, right, (((1,), (1,)), ((), ())), precision=HIGHEST, preferred_element_type=F32
    )


def load_sums(left, right):
    parts = split_faces(left * right)
    total = (parts[0] + parts[1]) + (parts[2] + parts[3]) + (parts[4] + parts[5])
    return matmul_nt_exact(jnp.ones((8, FACE), F32), total)


def living_kernel(counts, live_ref):
    live_ref[...] = jnp.full((8, FACE), (counts[0] > 0).astype(F32), F32)


def prepare_kernel(live_ref, loads, *sends):
    mark = live_ref[...]
    value = loads[0] * mark[0:1, 0:1]
    faces = [jnp.concatenate([face, mark], axis=0) for face in split_faces(value)]
    store_sends(sends, faces)


def copy_kernel(source, out):
    out[...] = source[...]


def halves_kernel(source, after, out, whole, turned):
    for c in range(COARSE // FACE):
        whole[c] = source[:, c * FACE : (c + 1) * FACE]
    for i in range(2):
        for c in range(COARSE // FACE):
            part = whole[c, pl.Slice(i, DEVICES, 2), :].T
            for h in range(2):
                turned[h, c * FACE : (c + 1) * FACE, :] = part[:, h * FACE : (h + 1) * FACE]
        for j in range(2):
            for h in range(2):
                high, low = halves(turned[h, pl.Slice(j, DEVICES, 2), :])
                first, start = j * DEVICES, i * DEVICES + h * FACE
                out[0, first : first + DEVICES, start : start + FACE] = high
                out[1, first : first + DEVICES, start : start + FACE] = low


def precondition(weight, residual, dirichlet):
    scaled = (weight * residual).astype(BF16)
    return weight * matmul(scaled, dirichlet[0])


def first_kernel(live_ref, loads, pairing, dirichlet, *refs):
    recvs, (resid, weight_ref, terms, dots), sends = refs[:6], refs[6:10], refs[10:]
    live = live_ref[0:1, 0:1]
    residual = live * (loads[0] * live + partner(recvs, pairing))
    multiplicity = live * (live + partner(recvs, pairing, slice(LOADS, LOADS + 8)))
    weight = live / jnp.maximum(multiplicity, 1.0)
    weight_ref[...] = weight
    resid[...] = residual
    applied = precondition(weight[0:1], residual, dirichlet)
    terms[...] = applied
    dots[...] = load_sums(residual, applied)
    store_sends(sends, split_faces(applied))


def corner_message(corner_map, corner_terms, scalars):
    place = coords()
    steps = ((0, 0, 0), (0, 1, 0), (1, 0, 0), (0, -1, 0), (-1, 0, 0), (0, 0, 1), None, (0, 0, -1))
    row = lax.broadcasted_iota(jnp.int32, (16, FACE), 0)
    target = jnp.full((16, FACE), -1, jnp.int32)
    for index, step in enumerate(steps):
        if step is not None:
            a, b, c = [(p + s + n) % n for p, s, n in zip(place, step, SIZES)]
            owned = 2 * ((a * SIZES[1] + b) * SIZES[2] + c)
            target = jnp.where(row == index, owned, target)
            target = jnp.where(row == index + 8, owned + 1, target)
    chosen = (target == corner_map[0:1, :]).astype(F32)
    sums = matmul_nt_exact(chosen, corner_terms)
    line = lax.broadcasted_iota(jnp.int32, (8, LOADS), 0)
    pair = [
        jnp.where(line == 6, scalar, sums[8 * i : 8 * i + 8]) for i, scalar in enumerate(scalars)
    ]
    messages = []
    for k in range(2):
        part = jnp.concatenate([value[:, k * HALF : (k + 1) * HALF] for value in pair], axis=1)
        messages.append(jnp.concatenate([part[2 * i : 2 * i + 2] for i in range(4)], axis=1))
    return messages


def send_message(out, messages):
    block = jnp.stack(messages * (SIZES[0] // 2))
    for i in range(SIDE):
        out[i * SIZES[0] : (i + 1) * SIZES[0]] = block


def second_kernel(live_ref, pairing, corner_map, schur, coupling, terms, dots, *refs):
    recvs, (z_ref, local_ref, out) = refs[:6], refs[6:]
    live = live_ref[0:1, 0:1]
    direction = live * (terms[...] + partner(recvs, pairing))
    dir_bf = direction.astype(BF16)
    local_terms = live * matmul(dir_bf, schur[0])
    corner_terms = live * matmul(dir_bf, coupling[0])
    z_ref[...] = direction
    local_ref[...] = local_terms
    curve = load_sums(direction, local_terms)
    send_message(out, corner_message(corner_map, corner_terms, (dots[0:1], curve[0:1])))


BY_COLUMN = ("gy", "gz", "region")


def combine_kernel(got, out, scratch):
    total = jnp.zeros((8, FACE), F32)

    def line(b, c, index):
        first = (b % SIZES[1] * SIZES[2] + c % SIZES[2]) * SIZES[0]
        return got[first : first + SIZES[0], index, :]

    for b in range(SIZES[1]):
        for c in range(SIZES[2]):
            here = line(b, c, 0)
            near = here + line(b - 1, c, 1)
            near = near + pltpu.roll(pltpu.roll(here, 1, 0) + line(b + 1, c, 1), 96, 1)
            near = near + pltpu.roll(pltpu.roll(here, 7, 0) + line(b, c - 1, 1), 64, 1)
            near = near + pltpu.roll(line(b, c + 1, 1), 32, 1)
            scratch[pl.Slice(b * SIZES[2] + c, SIZES[0], SIDE), :] = near
            total = total + here
    out[:, 0:DEVICES] = scratch[...].T[0:LOADS]
    scalars = jnp.broadcast_to(jnp.sum(total, axis=0, keepdims=True), (FACE, FACE)).T
    out[:, DEVICES : DEVICES + FACE] = scalars[96:128]


def coarse_sums(mine, other):
    odd = coords()[0] % 2 == 1
    low = jnp.where(odd, other[...], mine[...])
    high = jnp.where(odd, mine[...], other[...])
    both = [
        jnp.concatenate([low[i * HALF : (i + 1) * HALF], high[i * HALF : (i + 1) * HALF]], axis=0)
        for i in range(2)
    ]
    gathered = jnp.concatenate([value[:, 0:DEVICES] for value in both], axis=1)
    return gathered, [value[:, DEVICES : DEVICES + 1] for value in both]


def coarse_solve(inverse, gathered, corner_map, coupling):
    high, low = halves(gathered)
    both = matmul(jnp.concatenate([high, low], axis=0), inverse[0])
    solved = both[:LOADS] + (both[LOADS:] + matmul(high, inverse[1]))
    solved = solved.astype(BF16)
    row = lax.broadcasted_iota(jnp.int32, (COARSE, FACE), 0)
    index = corner_map[0:1, :]
    index = (index & 1) * DEVICES + (index >> 1)
    chosen = (row == index).astype(F32).astype(BF16)
    picked = matmul(solved, chosen).astype(BF16)
    return matmul_nt(picked, coupling[0]), solved.astype(F32)


def coarse_dot(solved, gathered):
    return jnp.sum(solved * gathered, axis=1, keepdims=True)


def lanes(*columns):
    lane = lax.broadcasted_iota(jnp.int32, (LOADS, FACE), 1)
    out = jnp.zeros((LOADS, FACE), F32)
    for index, value in enumerate(columns):
        out = jnp.where(lane == index, value, out)
    return out


def third_kernel(live_ref, corner_map, coupling, inverse, mine, other, local_ref, *refs):
    image_ref, gathered_ref, solved_ref, scalar_ref = refs[:4]
    sends = refs[4:]
    live = live_ref[0:1, 0:1]
    gathered, (resid_dot, local_curve) = coarse_sums(mine, other)
    coarse_terms, solved = coarse_solve(inverse, gathered, corner_map, coupling)
    image = live * (local_ref[...] + coarse_terms)
    curvature = local_curve + coarse_dot(solved, gathered)
    step_size = resid_dot / curvature
    image_ref[...] = image
    gathered_ref[...] = gathered
    solved_ref[...] = solved
    scalar_ref[...] = lanes(resid_dot, local_curve, step_size, curvature)
    store_sends(sends, split_faces(image))


def fourth_kernel(live_ref, pairing, dirichlet, resid, weight_ref, image_ref, scalar_ref, *refs):
    recvs, (resid_out, terms, dots), sends = refs[:6], refs[6:9], refs[9:]
    live = live_ref[0:1, 0:1]
    step_size = scalar_ref[:, 2:3]
    residual = resid[...] - step_size * (live * (image_ref[...] + partner(recvs, pairing)))
    resid_out[...] = residual
    applied = precondition(weight_ref[0:1, :], residual, dirichlet)
    terms[...] = applied
    dots[...] = load_sums(residual, applied)
    store_sends(sends, split_faces(applied))


def fifth_kernel(live_ref, pairing, corner_map, schur, coupling, terms, dots, *refs):
    recvs, (precond_ref, out) = refs[:6], refs[6:]
    live = live_ref[0:1, 0:1]
    precond = live * (terms[...] + partner(recvs, pairing))
    precond_ref[...] = precond
    high, low = halves(precond)
    local_terms = live * matmul(high, schur[0])
    both = matmul(jnp.concatenate([high, low], axis=0), coupling[0])
    corner_terms = live * (both[:LOADS] + both[LOADS:])
    square = load_sums(precond, local_terms)
    send_message(out, corner_message(corner_map, corner_terms, (dots[0:1], square[0:1])))


def sixth_kernel(
    live_ref, corner_map, schur, coupling, inverse, mine, other, gathered_ref, solved_ref,
    scalar_ref, z_ref, precond_ref, *refs
):
    direction_ref, image_ref, step_ref = refs[:3]
    sends = refs[3:]
    live = live_ref[0:1, 0:1]
    gathered, (new_dot, square) = coarse_sums(mine, other)
    beta = new_dot / scalar_ref[:, 0:1]
    cross = -beta * scalar_ref[:, 3:4] - coarse_dot(solved_ref[...], gathered)
    gathered = gathered + beta * gathered_ref[...]
    coarse_terms, solved = coarse_solve(inverse, gathered, corner_map, coupling)
    local_curve = square + beta * (2.0 * cross + beta * scalar_ref[:, 1:2])
    step_size = new_dot / (local_curve + coarse_dot(solved, gathered))
    first = z_ref[...]
    direction = precond_ref[...] + beta * first
    local_terms = matmul(direction.astype(BF16), schur[0])
    image = live * (local_terms + coarse_terms)
    image_ref[...] = image
    store_sends(sends, split_faces(image))
    step_ref[...] = lanes(step_size)
    direction_ref[...] = direction


def solution_kernel(scalar_ref, first, step_ref, direction, out):
    out[0] = scalar_ref[:, 2:3] * first[...] + step_ref[:, 0:1] * direction[...]


def seventh_kernel(live_ref, pairing, resid, image_ref, step_ref, *refs):
    recvs, (out,) = refs[:6], refs[6:]
    live = live_ref[0:1, 0:1]
    image = live * (image_ref[...] + partner(recvs, pairing))
    out[0] = resid[...] - step_ref[:, 0:1] * image


def call(kernel, shapes, *operands, scratch=(), cost=None, spec=VM):
    return pl.pallas_call(
        kernel,
        out_shape=[
            shape if hasattr(shape, "dtype") else jax.ShapeDtypeStruct(shape, F32)
            for shape in shapes
        ],
        in_specs=[spec] * len(operands),
        out_specs=[VM] * len(shapes),
        scratch_shapes=list(scratch),
        cost_estimate=cost,
        compiler_params=pltpu.CompilerParams(vmem_limit_bytes=32 << 20),
    )(*operands)


def matched(count, start):
    pairs = []
    for low in range(start, count, 2):
        high = (low + 1) % count
        pairs += [(low, high), (high, low)]
    return pairs


def exchange(sends):
    return [
        lax.ppermute(value, AXES[k // 2], matched(SIZES[k // 2], k % 2))
        for k, value in zip(ORDER, sends)
    ]


def total_sums(message):
    (mine,) = call(
        combine_kernel, [(LOADS, DEVICES + FACE)], lax.all_to_all(message, BY_COLUMN, 0, 0),
        scratch=[pltpu.VMEM((DEVICES, FACE), F32)],
    )
    return mine, lax.ppermute(mine, AXES[0], matched(SIZES[0], 0))


def local(loads, schur, dirichlet, coupling, coarse_inverse, pairing, corner_map, counts):
    vector = (LOADS, MULT)
    faces = [(LOADS, FACE)] * 6
    small = (8, LOADS)
    wide = (LOADS, FACE)

    pairing = pairing.reshape(6, 1, FACE)
    cost = pl.CostEstimate(flops=0, bytes_accessed=4 << 20, transcendentals=0)
    (live,) = call(living_kernel, [(8, FACE)], counts, spec=SMEM, cost=cost)
    sends = call(prepare_kernel, [(LOADS + 8, FACE)] * 6, live, loads)
    (dirichlet,) = call(copy_kernel, [jax.ShapeDtypeStruct(dirichlet.shape, BF16)], dirichlet)
    resid, weight, terms, dots, *sends = call(
        first_kernel, [vector, (8, MULT), vector, small] + faces,
        live, loads, pairing, dirichlet, *exchange(sends),
    )
    (inverse,) = call(
        halves_kernel, [jax.ShapeDtypeStruct((2, COARSE, COARSE), BF16)], coarse_inverse, dots,
        scratch=[
            pltpu.VMEM((COARSE // FACE, COARSE, FACE), F32),
            pltpu.VMEM((2, COARSE, FACE), F32),
        ],
    )
    first, local_terms, message = call(
        second_kernel, [vector, vector, (DEVICES, 2, FACE)],
        live, pairing, corner_map, schur, coupling, terms, dots, *exchange(sends),
    )
    image, gathered, solved, scalars, *sends = call(
        third_kernel, [vector, (LOADS, COARSE), (LOADS, COARSE), wide] + faces,
        live, corner_map, coupling, inverse, *total_sums(message), local_terms,
    )
    resid, terms, dots, *sends = call(
        fourth_kernel, [vector, vector, small] + faces,
        live, pairing, dirichlet, resid, weight, image, scalars, *exchange(sends),
    )
    precond, message = call(
        fifth_kernel, [vector, (DEVICES, 2, FACE)],
        live, pairing, corner_map, schur, coupling, terms, dots, *exchange(sends),
    )
    direction, image, step, *sends = call(
        sixth_kernel, [vector, vector, wide] + faces,
        live, corner_map, schur, coupling, inverse, *total_sums(message),
        gathered, solved, scalars, first, precond,
    )
    (solution_out,) = call(solution_kernel, [(1,) + vector], scalars, first, step, direction)
    (residual_out,) = call(
        seventh_kernel, [(1,) + vector],
        live, pairing, resid, image, step, *exchange(sends),
    )
    return solution_out, residual_out


def solution(mesh):
    block = P(AXES, None, None)
    in_specs = (block, block, block, block, P(), block, P(AXES, None), P(AXES))
    return jax.shard_map(
        local, mesh=mesh, in_specs=in_specs, out_specs=(block, block), check_vma=False
    )
```

```python
import jax
import jax.numpy as jnp
from jax import lax
from jax.experimental import pallas as pl
from jax.experimental.pallas import tpu as pltpu
from jax.sharding import PartitionSpec as P

AXES = ("region", "gy", "gz")
SIZES = (8, 8, 4)
F32 = jnp.float32
BF16 = jnp.bfloat16
LOADS = 32
FACE = 128
MULT = 768
COARSE = 512
SIDE = 32
HALF = 16
DEVICES = 256
HIGHEST = lax.Precision.HIGHEST
VM = pl.BlockSpec(memory_space=pltpu.VMEM)
SMEM = pl.BlockSpec(memory_space=pltpu.SMEM)


def matmul(left, right):
    return jnp.dot(left, right, preferred_element_type=F32)


def halves(value):
    high = value.astype(BF16)
    return high, (value - high.astype(F32)).astype(BF16)


def matmul_nt(left, right):
    return lax.dot_general(left, right, (((1,), (1,)), ((), ())), preferred_element_type=F32)


def coords():
    return [lax.axis_index(axis) for axis in AXES]


ORDER = (2, 3, 1, 4, 5, 0)


def store_sends(sends, faces):
    for e, place in enumerate(coords()):
        odd = place % 2 == 1
        first, second = ORDER.index(2 * e), ORDER.index(2 * e + 1)
        sends[first][...] = jnp.where(odd, faces[2 * e], faces[2 * e + 1])
        sends[second][...] = jnp.where(odd, faces[2 * e + 1], faces[2 * e])


def received_faces(recvs, rows):
    out = []
    for e, place in enumerate(coords()):
        odd = place % 2 == 1
        first = recvs[ORDER.index(2 * e)][rows, :]
        second = recvs[ORDER.index(2 * e + 1)][rows, :]
        lower = jnp.where(odd, first, second)
        upper = jnp.where(odd, second, first)
        out.append(jnp.where(place > 0, lower, 0.0))
        out.append(jnp.where(place < SIZES[e] - 1, upper, 0.0))
    return out


def partner(recvs, pairing, rows=slice(0, LOADS)):
    faces = received_faces(recvs, rows)
    parts = []
    for f in range(6):
        index = jnp.broadcast_to(pairing[f], faces[f].shape)
        parts.append(jnp.take_along_axis(faces[f], index, axis=1))
    return jnp.concatenate(parts, axis=1)


def split_faces(value):
    return [value[:, f * FACE : (f + 1) * FACE] for f in range(6)]


def matmul_nt_exact(left, right):
    return lax.dot_general(
        left, right, (((1,), (1,)), ((), ())), precision=HIGHEST, preferred_element_type=F32
    )


def load_sums(left, right):
    parts = split_faces(left * right)
    total = (parts[0] + parts[1]) + (parts[2] + parts[3]) + (parts[4] + parts[5])
    return matmul_nt_exact(jnp.ones((8, FACE), F32), total)


def living_kernel(counts, live_ref):
    live_ref[...] = jnp.full((8, FACE), (counts[0] > 0).astype(F32), F32)


def prepare_kernel(live_ref, loads, *sends):
    mark = live_ref[...]
    value = loads[0] * mark[0:1, 0:1]
    faces = [jnp.concatenate([face, mark], axis=0) for face in split_faces(value)]
    store_sends(sends, faces)


def copy_kernel(source, out):
    out[...] = source[...]


def halves_kernel(source, after, out, whole, turned):
    for c in range(COARSE // FACE):
        whole[c] = source[:, c * FACE : (c + 1) * FACE]
    for i in range(2):
        for c in range(COARSE // FACE):
            part = whole[c, pl.Slice(i, DEVICES, 2), :].T
            for h in range(2):
                turned[h, c * FACE : (c + 1) * FACE, :] = part[:, h * FACE : (h + 1) * FACE]
        for j in range(2):
            for h in range(2):
                high, low = halves(turned[h, pl.Slice(j, DEVICES, 2), :])
                first, start = j * DEVICES, i * DEVICES + h * FACE
                out[0, first : first + DEVICES, start : start + FACE] = high
                out[1, first : first + DEVICES, start : start + FACE] = low


def precondition(weight, residual, dirichlet):
    scaled = (weight * residual).astype(BF16)
    return weight * matmul(scaled, dirichlet[0])


def first_kernel(live_ref, loads, pairing, dirichlet, *refs):
    recvs, (resid, weight_ref, terms, dots), sends = refs[:6], refs[6:10], refs[10:]
    live = live_ref[0:1, 0:1]
    residual = live * (loads[0] * live + partner(recvs, pairing))
    multiplicity = live * (live + partner(recvs, pairing, slice(LOADS, LOADS + 8)))
    weight = live / jnp.maximum(multiplicity, 1.0)
    weight_ref[...] = weight
    resid[...] = residual
    applied = precondition(weight[0:1], residual, dirichlet)
    terms[...] = applied
    dots[...] = load_sums(residual, applied)
    store_sends(sends, split_faces(applied))


def corner_message(corner_map, corner_terms, scalars):
    place = coords()
    steps = ((0, 0, 0), (0, 1, 0), (1, 0, 0), (0, -1, 0), (-1, 0, 0), (0, 0, 1), None, (0, 0, -1))
    row = lax.broadcasted_iota(jnp.int32, (16, FACE), 0)
    target = jnp.full((16, FACE), -1, jnp.int32)
    for index, step in enumerate(steps):
        if step is not None:
            a, b, c = [(p + s + n) % n for p, s, n in zip(place, step, SIZES)]
            owned = 2 * ((a * SIZES[1] + b) * SIZES[2] + c)
            target = jnp.where(row == index, owned, target)
            target = jnp.where(row == index + 8, owned + 1, target)
    chosen = (target == corner_map[0:1, :]).astype(F32)
    sums = matmul_nt_exact(chosen, corner_terms)
    line = lax.broadcasted_iota(jnp.int32, (8, LOADS), 0)
    pair = [
        jnp.where(line == 6, scalar, sums[8 * i : 8 * i + 8]) for i, scalar in enumerate(scalars)
    ]
    messages = []
    for k in range(2):
        part = jnp.concatenate([value[:, k * HALF : (k + 1) * HALF] for value in pair], axis=1)
        messages.append(jnp.concatenate([part[2 * i : 2 * i + 2] for i in range(4)], axis=1))
    return messages


def send_message(out, messages):
    block = jnp.stack(messages * (SIZES[0] // 2))
    for i in range(SIDE):
        out[i * SIZES[0] : (i + 1) * SIZES[0]] = block


def second_kernel(live_ref, pairing, corner_map, schur, coupling, terms, dots, *refs):
    recvs, (z_ref, local_ref, out) = refs[:6], refs[6:]
    live = live_ref[0:1, 0:1]
    direction = live * (terms[...] + partner(recvs, pairing))
    dir_bf = direction.astype(BF16)
    local_terms = live * matmul(dir_bf, schur[0])
    corner_terms = live * matmul(dir_bf, coupling[0])
    z_ref[...] = direction
    local_ref[...] = local_terms
    curve = load_sums(direction, local_terms)
    send_message(out, corner_message(corner_map, corner_terms, (dots[0:1], curve[0:1])))


BY_COLUMN = ("gy", "gz", "region")


def combine_kernel(got, out, scratch):
    total = jnp.zeros((8, FACE), F32)

    def line(b, c, index):
        first = (b % SIZES[1] * SIZES[2] + c % SIZES[2]) * SIZES[0]
        return got[first : first + SIZES[0], index, :]

    for b in range(SIZES[1]):
        for c in range(SIZES[2]):
            here = line(b, c, 0)
            near = here + line(b - 1, c, 1)
            near = near + pltpu.roll(pltpu.roll(here, 1, 0) + line(b + 1, c, 1), 96, 1)
            near = near + pltpu.roll(pltpu.roll(here, 7, 0) + line(b, c - 1, 1), 64, 1)
            near = near + pltpu.roll(line(b, c + 1, 1), 32, 1)
            scratch[pl.Slice(b * SIZES[2] + c, SIZES[0], SIDE), :] = near
            total = total + here
    out[:, 0:DEVICES] = scratch[...].T[0:LOADS]
    scalars = jnp.broadcast_to(jnp.sum(total, axis=0, keepdims=True), (FACE, FACE)).T
    out[:, DEVICES : DEVICES + FACE] = scalars[96:128]


def coarse_sums(mine, other):
    odd = coords()[0] % 2 == 1
    low = jnp.where(odd, other[...], mine[...])
    high = jnp.where(odd, mine[...], other[...])
    both = [
        jnp.concatenate([low[i * HALF : (i + 1) * HALF], high[i * HALF : (i + 1) * HALF]], axis=0)
        for i in range(2)
    ]
    gathered = jnp.concatenate([value[:, 0:DEVICES] for value in both], axis=1)
    return gathered, [value[:, DEVICES : DEVICES + 1] for value in both]


def coarse_solve(inverse, gathered, corner_map, coupling):
    high, low = halves(gathered)
    both = matmul(jnp.concatenate([high, low], axis=0), inverse[0])
    solved = both[:LOADS] + (both[LOADS:] + matmul(high, inverse[1]))
    solved = solved.astype(BF16)
    row = lax.broadcasted_iota(jnp.int32, (COARSE, FACE), 0)
    index = corner_map[0:1, :]
    index = (index & 1) * DEVICES + (index >> 1)
    chosen = (row == index).astype(F32).astype(BF16)
    picked = matmul(solved, chosen).astype(BF16)
    return matmul_nt(picked, coupling[0]), solved.astype(F32)


def coarse_dot(solved, gathered):
    return jnp.sum(solved * gathered, axis=1, keepdims=True)


def lanes(*columns):
    lane = lax.broadcasted_iota(jnp.int32, (LOADS, FACE), 1)
    out = jnp.zeros((LOADS, FACE), F32)
    for index, value in enumerate(columns):
        out = jnp.where(lane == index, value, out)
    return out


def third_kernel(live_ref, corner_map, coupling, inverse, mine, other, local_ref, *refs):
    image_ref, gathered_ref, solved_ref, scalar_ref = refs[:4]
    sends = refs[4:]
    live = live_ref[0:1, 0:1]
    gathered, (resid_dot, local_curve) = coarse_sums(mine, other)
    coarse_terms, solved = coarse_solve(inverse, gathered, corner_map, coupling)
    image = live * (local_ref[...] + coarse_terms)
    curvature = local_curve + coarse_dot(solved, gathered)
    step_size = resid_dot / curvature
    image_ref[...] = image
    gathered_ref[...] = gathered
    solved_ref[...] = solved
    scalar_ref[...] = lanes(resid_dot, local_curve, step_size, curvature)
    store_sends(sends, split_faces(image))


def fourth_kernel(live_ref, pairing, dirichlet, resid, weight_ref, image_ref, scalar_ref, *refs):
    recvs, (resid_out, terms, dots), sends = refs[:6], refs[6:9], refs[9:]
    live = live_ref[0:1, 0:1]
    step_size = scalar_ref[:, 2:3]
    residual = resid[...] - step_size * (live * (image_ref[...] + partner(recvs, pairing)))
    resid_out[...] = residual
    applied = precondition(weight_ref[0:1, :], residual, dirichlet)
    terms[...] = applied
    dots[...] = load_sums(residual, applied)
    store_sends(sends, split_faces(applied))


def fifth_kernel(live_ref, pairing, corner_map, schur, coupling, terms, dots, *refs):
    recvs, (precond_ref, out) = refs[:6], refs[6:]
    live = live_ref[0:1, 0:1]
    precond = live * (terms[...] + partner(recvs, pairing))
    precond_ref[...] = precond
    high, low = halves(precond)
    local_terms = live * matmul(high, schur[0])
    both = matmul(jnp.concatenate([high, low], axis=0), coupling[0])
    corner_terms = live * (both[:LOADS] + both[LOADS:])
    square = load_sums(precond, local_terms)
    send_message(out, corner_message(corner_map, corner_terms, (dots[0:1], square[0:1])))


def sixth_kernel(
    live_ref, corner_map, schur, coupling, inverse, mine, other, gathered_ref, solved_ref,
    scalar_ref, z_ref, precond_ref, *refs
):
    direction_ref, image_ref, step_ref = refs[:3]
    sends = refs[3:]
    live = live_ref[0:1, 0:1]
    gathered, (new_dot, square) = coarse_sums(mine, other)
    beta = new_dot / scalar_ref[:, 0:1]
    cross = -beta * scalar_ref[:, 3:4] - coarse_dot(solved_ref[...], gathered)
    gathered = gathered + beta * gathered_ref[...]
    coarse_terms, solved = coarse_solve(inverse, gathered, corner_map, coupling)
    local_curve = square + beta * (2.0 * cross + beta * scalar_ref[:, 1:2])
    step_size = new_dot / (local_curve + coarse_dot(solved, gathered))
    first = z_ref[...]
    direction = precond_ref[...] + beta * first
    local_terms = matmul(direction.astype(BF16), schur[0])
    image = live * (local_terms + coarse_terms)
    image_ref[...] = image
    store_sends(sends, split_faces(image))
    step_ref[...] = lanes(step_size)
    direction_ref[...] = direction


def solution_kernel(scalar_ref, first, step_ref, direction, out):
    out[0] = scalar_ref[:, 2:3] * first[...] + step_ref[:, 0:1] * direction[...]


def seventh_kernel(live_ref, pairing, resid, image_ref, step_ref, *refs):
    recvs, (out,) = refs[:6], refs[6:]
    live = live_ref[0:1, 0:1]
    image = live * (image_ref[...] + partner(recvs, pairing))
    out[0] = resid[...] - step_ref[:, 0:1] * image


def call(kernel, shapes, *operands, scratch=(), cost=None, spec=VM):
    return pl.pallas_call(
        kernel,
        out_shape=[
            shape if hasattr(shape, "dtype") else jax.ShapeDtypeStruct(shape, F32)
            for shape in shapes
        ],
        in_specs=[spec] * len(operands),
        out_specs=[VM] * len(shapes),
        scratch_shapes=list(scratch),
        cost_estimate=cost,
        compiler_params=pltpu.CompilerParams(vmem_limit_bytes=32 << 20),
    )(*operands)


def pairs(axis, start):
    out = []
    for a in range(SIZES[0]):
        for b in range(SIZES[1]):
            for c in range(SIZES[2]):
                here, there = (a, b, c), [a, b, c]
                if start and here[axis] in (0, SIZES[axis] - 1):
                    other = 1 if axis == 0 else 0
                    there[other] = here[other] ^ 1
                else:
                    there[axis] += 1 if (here[axis] - start) % 2 == 0 else -1
                place = [(p * SIZES[1] + q) * SIZES[2] + r for p, q, r in (here, there)]
                out.append(tuple(place))
    return out


def exchange(sends):
    return [
        lax.ppermute(value, AXES, pairs(k // 2, k % 2)) for k, value in zip(ORDER, sends)
    ]


def total_sums(message):
    (mine,) = call(
        combine_kernel, [(LOADS, DEVICES + FACE)], lax.all_to_all(message, BY_COLUMN, 0, 0),
        scratch=[pltpu.VMEM((DEVICES, FACE), F32)],
    )
    return mine, lax.ppermute(mine, AXES, pairs(0, 0))


def local(loads, schur, dirichlet, coupling, coarse_inverse, pairing, corner_map, counts):
    vector = (LOADS, MULT)
    faces = [(LOADS, FACE)] * 6
    small = (8, LOADS)
    wide = (LOADS, FACE)

    pairing = pairing.reshape(6, 1, FACE)
    cost = pl.CostEstimate(flops=0, bytes_accessed=4 << 20, transcendentals=0)
    (live,) = call(living_kernel, [(8, FACE)], counts, spec=SMEM, cost=cost)
    sends = call(prepare_kernel, [(LOADS + 8, FACE)] * 6, live, loads)
    (dirichlet,) = call(copy_kernel, [jax.ShapeDtypeStruct(dirichlet.shape, BF16)], dirichlet)
    resid, weight, terms, dots, *sends = call(
        first_kernel, [vector, (8, MULT), vector, small] + faces,
        live, loads, pairing, dirichlet, *exchange(sends),
    )
    (inverse,) = call(
        halves_kernel, [jax.ShapeDtypeStruct((2, COARSE, COARSE), BF16)], coarse_inverse, dots,
        scratch=[
            pltpu.VMEM((COARSE // FACE, COARSE, FACE), F32),
            pltpu.VMEM((2, COARSE, FACE), F32),
        ],
    )
    first, local_terms, message = call(
        second_kernel, [vector, vector, (DEVICES, 2, FACE)],
        live, pairing, corner_map, schur, coupling, terms, dots, *exchange(sends),
    )
    image, gathered, solved, scalars, *sends = call(
        third_kernel, [vector, (LOADS, COARSE), (LOADS, COARSE), wide] + faces,
        live, corner_map, coupling, inverse, *total_sums(message), local_terms,
    )
    resid, terms, dots, *sends = call(
        fourth_kernel, [vector, vector, small] + faces,
        live, pairing, dirichlet, resid, weight, image, scalars, *exchange(sends),
    )
    precond, message = call(
        fifth_kernel, [vector, (DEVICES, 2, FACE)],
        live, pairing, corner_map, schur, coupling, terms, dots, *exchange(sends),
    )
    direction, image, step, *sends = call(
        sixth_kernel, [vector, vector, wide] + faces,
        live, corner_map, schur, coupling, inverse, *total_sums(message),
        gathered, solved, scalars, first, precond,
    )
    (solution_out,) = call(solution_kernel, [(1,) + vector], scalars, first, step, direction)
    (residual_out,) = call(
        seventh_kernel, [(1,) + vector],
        live, pairing, resid, image, step, *exchange(sends),
    )
    return solution_out, residual_out


def solution(mesh):
    block = P(AXES, None, None)
    in_specs = (block, block, block, block, P(), block, P(AXES, None), P(AXES))
    return jax.shard_map(
        local, mesh=mesh, in_specs=in_specs, out_specs=(block, block), check_vma=False
    )
```

```python
import jax
import jax.numpy as jnp
from jax import lax
from jax.experimental import pallas as pl
from jax.experimental.pallas import tpu as pltpu
from jax.sharding import PartitionSpec as P

AXES = ("region", "gy", "gz")
SIZES = (8, 8, 4)
F32 = jnp.float32
BF16 = jnp.bfloat16
LOADS = 32
FACE = 128
MULT = 768
COARSE = 512
SIDE = 32
HALF = 16
DEVICES = 256
HIGHEST = lax.Precision.HIGHEST
VM = pl.BlockSpec(memory_space=pltpu.VMEM)
SMEM = pl.BlockSpec(memory_space=pltpu.SMEM)


def matmul(left, right):
    return jnp.dot(left, right, preferred_element_type=F32)


def halves(value):
    high = value.astype(BF16)
    return high, (value - high.astype(F32)).astype(BF16)


def matmul_nt(left, right):
    return lax.dot_general(left, right, (((1,), (1,)), ((), ())), preferred_element_type=F32)


def coords():
    return [lax.axis_index(axis) for axis in AXES]


ORDER = (2, 3, 1, 4, 5, 0)


def store_sends(sends, faces):
    for e, place in enumerate(coords()):
        odd = place % 2 == 1
        first, second = ORDER.index(2 * e), ORDER.index(2 * e + 1)
        sends[first][...] = jnp.where(odd, faces[2 * e], faces[2 * e + 1])
        sends[second][...] = jnp.where(odd, faces[2 * e + 1], faces[2 * e])


def received_faces(recvs, rows):
    out = []
    for e, place in enumerate(coords()):
        odd = place % 2 == 1
        first = recvs[ORDER.index(2 * e)][rows, :]
        second = recvs[ORDER.index(2 * e + 1)][rows, :]
        lower = jnp.where(odd, first, second)
        upper = jnp.where(odd, second, first)
        out.append(jnp.where(place > 0, lower, 0.0))
        out.append(jnp.where(place < SIZES[e] - 1, upper, 0.0))
    return out


def partner(recvs, pairing, rows=slice(0, LOADS)):
    faces = received_faces(recvs, rows)
    parts = []
    for f in range(6):
        index = jnp.broadcast_to(pairing[f], faces[f].shape)
        parts.append(jnp.take_along_axis(faces[f], index, axis=1))
    return jnp.concatenate(parts, axis=1)


def split_faces(value):
    return [value[:, f * FACE : (f + 1) * FACE] for f in range(6)]


def matmul_nt_exact(left, right):
    return lax.dot_general(
        left, right, (((1,), (1,)), ((), ())), precision=HIGHEST, preferred_element_type=F32
    )


def load_sums(left, right):
    parts = split_faces(left * right)
    total = (parts[0] + parts[1]) + (parts[2] + parts[3]) + (parts[4] + parts[5])
    return matmul_nt_exact(jnp.ones((8, FACE), F32), total)


def living_kernel(counts, live_ref):
    live_ref[...] = jnp.full((8, FACE), (counts[0] > 0).astype(F32), F32)


def prepare_kernel(live_ref, loads, value_ref, *sends):
    mark = live_ref[...]
    value = loads[0] * mark[0:1, 0:1]
    value_ref[...] = value
    faces = [jnp.concatenate([face, mark], axis=0) for face in split_faces(value)]
    store_sends(sends, faces)


def copy_kernel(source, out):
    out[...] = source[...]


def halves_kernel(source, after, out, whole, turned):
    for c in range(COARSE // FACE):
        whole[c] = source[:, c * FACE : (c + 1) * FACE]
    for i in range(2):
        for c in range(COARSE // FACE):
            part = whole[c, pl.Slice(i, DEVICES, 2), :].T
            for h in range(2):
                turned[h, c * FACE : (c + 1) * FACE, :] = part[:, h * FACE : (h + 1) * FACE]
        for j in range(2):
            for h in range(2):
                high, low = halves(turned[h, pl.Slice(j, DEVICES, 2), :])
                first, start = j * DEVICES, i * DEVICES + h * FACE
                out[0, first : first + DEVICES, start : start + FACE] = high
                out[1, first : first + DEVICES, start : start + FACE] = low


def precondition(weight, residual, dirichlet):
    scaled = (weight * residual).astype(BF16)
    return weight * matmul(scaled, dirichlet[0])


def first_kernel(live_ref, value_ref, pairing, dirichlet, *refs):
    recvs, (resid, weight_ref, terms, dots), sends = refs[:6], refs[6:10], refs[10:]
    live = live_ref[0:1, 0:1]
    residual = live * (value_ref[...] + partner(recvs, pairing))
    multiplicity = live * (live + partner(recvs, pairing, slice(LOADS, LOADS + 8)))
    weight = live / jnp.maximum(multiplicity, 1.0)
    weight_ref[...] = weight
    resid[...] = residual
    applied = precondition(weight[0:1], residual, dirichlet)
    terms[...] = applied
    dots[...] = load_sums(residual, applied)
    store_sends(sends, split_faces(applied))


def corner_message(corner_map, corner_terms, scalars):
    place = coords()
    steps = ((0, 0, 0), (0, 1, 0), (1, 0, 0), (0, -1, 0), (-1, 0, 0), (0, 0, 1), None, (0, 0, -1))
    row = lax.broadcasted_iota(jnp.int32, (16, FACE), 0)
    target = jnp.full((16, FACE), -1, jnp.int32)
    for index, step in enumerate(steps):
        if step is not None:
            a, b, c = [(p + s + n) % n for p, s, n in zip(place, step, SIZES)]
            owned = 2 * ((a * SIZES[1] + b) * SIZES[2] + c)
            target = jnp.where(row == index, owned, target)
            target = jnp.where(row == index + 8, owned + 1, target)
    chosen = (target == corner_map[0:1, :]).astype(F32)
    sums = matmul_nt_exact(chosen, corner_terms)
    line = lax.broadcasted_iota(jnp.int32, (8, LOADS), 0)
    pair = [
        jnp.where(line == 6, scalar, sums[8 * i : 8 * i + 8]) for i, scalar in enumerate(scalars)
    ]
    messages = []
    for k in range(2):
        part = jnp.concatenate([value[:, k * HALF : (k + 1) * HALF] for value in pair], axis=1)
        messages.append(jnp.concatenate([part[2 * i : 2 * i + 2] for i in range(4)], axis=1))
    return messages


def send_message(out, messages):
    block = jnp.concatenate(messages * 4, axis=0)
    for i in range(2 * DEVICES // 16):
        out[i * 16 : (i + 1) * 16] = block


def second_kernel(live_ref, pairing, corner_map, schur, coupling, terms, dots, *refs):
    recvs, (z_ref, local_ref, out) = refs[:6], refs[6:]
    live = live_ref[0:1, 0:1]
    direction = live * (terms[...] + partner(recvs, pairing))
    dir_bf = direction.astype(BF16)
    local_terms = live * matmul(dir_bf, schur[0])
    corner_terms = live * matmul(dir_bf, coupling[0])
    z_ref[...] = direction
    local_ref[...] = local_terms
    curve = load_sums(direction, local_terms)
    send_message(out, corner_message(corner_map, corner_terms, (dots[0:1], curve[0:1])))


BY_COLUMN = ("gy", "gz", "region")


def combine_kernel(got, out, scratch):
    total = jnp.zeros((8, FACE), F32)

    def line(b, c, index):
        first = (b % SIZES[1] * SIZES[2] + c % SIZES[2]) * SIZES[0]
        return got[pl.Slice(2 * first + index, SIZES[0], 2), :]

    for b in range(SIZES[1]):
        for c in range(SIZES[2]):
            here = line(b, c, 0)
            near = here + line(b - 1, c, 1)
            near = near + pltpu.roll(pltpu.roll(here, 1, 0) + line(b + 1, c, 1), 96, 1)
            near = near + pltpu.roll(pltpu.roll(here, 7, 0) + line(b, c - 1, 1), 64, 1)
            near = near + pltpu.roll(line(b, c + 1, 1), 32, 1)
            scratch[pl.Slice(b * SIZES[2] + c, SIZES[0], SIDE), :] = near
            total = total + here
    out[:, 0:DEVICES] = scratch[...].T[0:LOADS]
    scalars = jnp.broadcast_to(jnp.sum(total, axis=0, keepdims=True), (FACE, FACE)).T
    out[:, DEVICES : DEVICES + FACE] = scalars[96:128]


def coarse_sums(mine, other):
    odd = coords()[0] % 2 == 1
    low = jnp.where(odd, other[...], mine[...])
    high = jnp.where(odd, mine[...], other[...])
    both = [
        jnp.concatenate([low[i * HALF : (i + 1) * HALF], high[i * HALF : (i + 1) * HALF]], axis=0)
        for i in range(2)
    ]
    gathered = jnp.concatenate([value[:, 0:DEVICES] for value in both], axis=1)
    return gathered, [value[:, DEVICES : DEVICES + 1] for value in both]


def coarse_solve(inverse, gathered, corner_map, coupling):
    high, low = halves(gathered)
    both = matmul(jnp.concatenate([high, low], axis=0), inverse[0])
    solved = both[:LOADS] + (both[LOADS:] + matmul(high, inverse[1]))
    solved = solved.astype(BF16)
    row = lax.broadcasted_iota(jnp.int32, (COARSE, FACE), 0)
    index = corner_map[0:1, :]
    index = (index & 1) * DEVICES + (index >> 1)
    chosen = (row == index).astype(F32).astype(BF16)
    picked = matmul(solved, chosen).astype(BF16)
    return matmul_nt(picked, coupling[0]), solved.astype(F32)


def coarse_dot(solved, gathered):
    return jnp.sum(solved * gathered, axis=1, keepdims=True)


def lanes(*columns):
    lane = lax.broadcasted_iota(jnp.int32, (LOADS, FACE), 1)
    out = jnp.zeros((LOADS, FACE), F32)
    for index, value in enumerate(columns):
        out = jnp.where(lane == index, value, out)
    return out


def third_kernel(live_ref, corner_map, coupling, inverse, mine, other, local_ref, *refs):
    image_ref, gathered_ref, solved_ref, scalar_ref = refs[:4]
    sends = refs[4:]
    live = live_ref[0:1, 0:1]
    gathered, (resid_dot, local_curve) = coarse_sums(mine, other)
    coarse_terms, solved = coarse_solve(inverse, gathered, corner_map, coupling)
    image = live * (local_ref[...] + coarse_terms)
    curvature = local_curve + coarse_dot(solved, gathered)
    step_size = resid_dot / curvature
    image_ref[...] = image
    gathered_ref[...] = gathered
    solved_ref[...] = solved
    scalar_ref[...] = lanes(resid_dot, local_curve, step_size, curvature)
    store_sends(sends, split_faces(image))


def fourth_kernel(live_ref, pairing, dirichlet, resid, weight_ref, image_ref, scalar_ref, *refs):
    recvs, (resid_out, terms, dots), sends = refs[:6], refs[6:9], refs[9:]
    live = live_ref[0:1, 0:1]
    step_size = scalar_ref[:, 2:3]
    residual = resid[...] - step_size * (live * (image_ref[...] + partner(recvs, pairing)))
    resid_out[...] = residual
    applied = precondition(weight_ref[0:1, :], residual, dirichlet)
    terms[...] = applied
    dots[...] = load_sums(residual, applied)
    store_sends(sends, split_faces(applied))


def fifth_kernel(live_ref, pairing, corner_map, schur, coupling, terms, dots, *refs):
    recvs, (precond_ref, out) = refs[:6], refs[6:]
    live = live_ref[0:1, 0:1]
    precond = live * (terms[...] + partner(recvs, pairing))
    precond_ref[...] = precond
    high, low = halves(precond)
    local_terms = live * matmul(high, schur[0])
    both = matmul(jnp.concatenate([high, low], axis=0), coupling[0])
    corner_terms = live * (both[:LOADS] + both[LOADS:])
    square = load_sums(precond, local_terms)
    send_message(out, corner_message(corner_map, corner_terms, (dots[0:1], square[0:1])))


def sixth_kernel(
    live_ref, corner_map, schur, coupling, inverse, mine, other, gathered_ref, solved_ref,
    scalar_ref, z_ref, precond_ref, *refs
):
    direction_ref, image_ref, step_ref = refs[:3]
    sends = refs[3:]
    live = live_ref[0:1, 0:1]
    gathered, (new_dot, square) = coarse_sums(mine, other)
    beta = new_dot / scalar_ref[:, 0:1]
    cross = -beta * scalar_ref[:, 3:4] - coarse_dot(solved_ref[...], gathered)
    gathered = gathered + beta * gathered_ref[...]
    coarse_terms, solved = coarse_solve(inverse, gathered, corner_map, coupling)
    local_curve = square + beta * (2.0 * cross + beta * scalar_ref[:, 1:2])
    step_size = new_dot / (local_curve + coarse_dot(solved, gathered))
    first = z_ref[...]
    direction = precond_ref[...] + beta * first
    local_terms = matmul(direction.astype(BF16), schur[0])
    image = live * (local_terms + coarse_terms)
    image_ref[...] = image
    store_sends(sends, split_faces(image))
    step_ref[...] = lanes(step_size)
    direction_ref[...] = direction


def solution_kernel(scalar_ref, first, step_ref, direction, out):
    out[0] = scalar_ref[:, 2:3] * first[...] + step_ref[:, 0:1] * direction[...]


def seventh_kernel(live_ref, pairing, resid, image_ref, step_ref, *refs):
    recvs, (out,) = refs[:6], refs[6:]
    live = live_ref[0:1, 0:1]
    image = live * (image_ref[...] + partner(recvs, pairing))
    out[0] = resid[...] - step_ref[:, 0:1] * image


def call(kernel, shapes, *operands, scratch=(), cost=None, spec=VM):
    return pl.pallas_call(
        kernel,
        out_shape=[
            shape if hasattr(shape, "dtype") else jax.ShapeDtypeStruct(shape, F32)
            for shape in shapes
        ],
        in_specs=[spec] * len(operands),
        out_specs=[VM] * len(shapes),
        scratch_shapes=list(scratch),
        cost_estimate=cost,
        compiler_params=pltpu.CompilerParams(vmem_limit_bytes=32 << 20),
    )(*operands)


def pairs(axis, start):
    out = []
    for a in range(SIZES[0]):
        for b in range(SIZES[1]):
            for c in range(SIZES[2]):
                here, there = (a, b, c), [a, b, c]
                if start and here[axis] in (0, SIZES[axis] - 1):
                    other = 1 if axis == 0 else 0
                    there[other] = here[other] ^ 1
                else:
                    there[axis] += 1 if (here[axis] - start) % 2 == 0 else -1
                place = [(p * SIZES[1] + q) * SIZES[2] + r for p, q, r in (here, there)]
                out.append(tuple(place))
    return out


def exchange(sends):
    return [
        lax.ppermute(value, AXES, pairs(k // 2, k % 2)) for k, value in zip(ORDER, sends)
    ]


def total_sums(message):
    message = lax.all_to_all(message.reshape(DEVICES, 2, FACE), BY_COLUMN, 0, 0)
    (mine,) = call(
        combine_kernel, [(LOADS, DEVICES + FACE)], message.reshape(2 * DEVICES, FACE),
        scratch=[pltpu.VMEM((DEVICES, FACE), F32)],
    )
    return mine, lax.ppermute(mine, AXES, pairs(0, 0))


def local(loads, schur, dirichlet, coupling, coarse_inverse, pairing, corner_map, counts):
    vector = (LOADS, MULT)
    faces = [(LOADS, FACE)] * 6
    small = (8, LOADS)
    wide = (LOADS, FACE)

    pairing = pairing.reshape(6, 1, FACE)
    cost = pl.CostEstimate(flops=0, bytes_accessed=4 << 20, transcendentals=0)
    (live,) = call(living_kernel, [(8, FACE)], counts, spec=SMEM, cost=cost)
    value, *sends = call(prepare_kernel, [vector] + [(LOADS + 8, FACE)] * 6, live, loads)
    (dirichlet,) = call(copy_kernel, [jax.ShapeDtypeStruct(dirichlet.shape, BF16)], dirichlet)
    resid, weight, terms, dots, *sends = call(
        first_kernel, [vector, (8, MULT), vector, small] + faces,
        live, value, pairing, dirichlet, *exchange(sends),
    )
    (inverse,) = call(
        halves_kernel, [jax.ShapeDtypeStruct((2, COARSE, COARSE), BF16)], coarse_inverse, dots,
        scratch=[
            pltpu.VMEM((COARSE // FACE, COARSE, FACE), F32),
            pltpu.VMEM((2, COARSE, FACE), F32),
        ],
    )
    first, local_terms, message = call(
        second_kernel, [vector, vector, (2 * DEVICES, FACE)],
        live, pairing, corner_map, schur, coupling, terms, dots, *exchange(sends),
    )
    image, gathered, solved, scalars, *sends = call(
        third_kernel, [vector, (LOADS, COARSE), (LOADS, COARSE), wide] + faces,
        live, corner_map, coupling, inverse, *total_sums(message), local_terms,
    )
    resid, terms, dots, *sends = call(
        fourth_kernel, [vector, vector, small] + faces,
        live, pairing, dirichlet, resid, weight, image, scalars, *exchange(sends),
    )
    precond, message = call(
        fifth_kernel, [vector, (2 * DEVICES, FACE)],
        live, pairing, corner_map, schur, coupling, terms, dots, *exchange(sends),
    )
    direction, image, step, *sends = call(
        sixth_kernel, [vector, vector, wide] + faces,
        live, corner_map, schur, coupling, inverse, *total_sums(message),
        gathered, solved, scalars, first, precond,
    )
    (solution_out,) = call(solution_kernel, [(1,) + vector], scalars, first, step, direction)
    (residual_out,) = call(
        seventh_kernel, [(1,) + vector],
        live, pairing, resid, image, step, *exchange(sends),
    )
    return solution_out, residual_out


def solution(mesh):
    block = P(AXES, None, None)
    in_specs = (block, block, block, block, P(), block, P(AXES, None), P(AXES))
    return jax.shard_map(
        local, mesh=mesh, in_specs=in_specs, out_specs=(block, block), check_vma=False
    )
```

```python
import jax
import jax.numpy as jnp
from jax import lax
from jax.experimental import pallas as pl
from jax.experimental.pallas import tpu as pltpu
from jax.sharding import PartitionSpec as P

AXES = ("region", "gy", "gz")
SIZES = (8, 8, 4)
F32 = jnp.float32
BF16 = jnp.bfloat16
LOADS = 32
FACE = 128
MULT = 768
COARSE = 512
SIDE = 32
HALF = 16
DEVICES = 256
HIGHEST = lax.Precision.HIGHEST
VM = pl.BlockSpec(memory_space=pltpu.VMEM)
SMEM = pl.BlockSpec(memory_space=pltpu.SMEM)


def matmul(left, right):
    return jnp.dot(left, right, preferred_element_type=F32)


def halves(value):
    high = value.astype(BF16)
    return high, (value - high.astype(F32)).astype(BF16)


def matmul_nt(left, right):
    return lax.dot_general(left, right, (((1,), (1,)), ((), ())), preferred_element_type=F32)


def coords():
    return [lax.axis_index(axis) for axis in AXES]


ORDER = (3, 2, 1, 4, 5, 0)


def store_sends(sends, faces):
    for e, place in enumerate(coords()):
        odd = place % 2 == 1
        first, second = ORDER.index(2 * e), ORDER.index(2 * e + 1)
        sends[first][...] = jnp.where(odd, faces[2 * e], faces[2 * e + 1])
        sends[second][...] = jnp.where(odd, faces[2 * e + 1], faces[2 * e])


def received_faces(recvs, rows):
    out = []
    for e, place in enumerate(coords()):
        odd = place % 2 == 1
        first = recvs[ORDER.index(2 * e)][rows, :]
        second = recvs[ORDER.index(2 * e + 1)][rows, :]
        lower = jnp.where(odd, first, second)
        upper = jnp.where(odd, second, first)
        out.append(jnp.where(place > 0, lower, 0.0))
        out.append(jnp.where(place < SIZES[e] - 1, upper, 0.0))
    return out


def partner(recvs, pairing, rows=slice(0, LOADS)):
    faces = received_faces(recvs, rows)
    parts = []
    for f in range(6):
        index = jnp.broadcast_to(pairing[f], faces[f].shape)
        parts.append(jnp.take_along_axis(faces[f], index, axis=1))
    return jnp.concatenate(parts, axis=1)


def split_faces(value):
    return [value[:, f * FACE : (f + 1) * FACE] for f in range(6)]


def matmul_nt_exact(left, right):
    return lax.dot_general(
        left, right, (((1,), (1,)), ((), ())), precision=HIGHEST, preferred_element_type=F32
    )


def load_sums(left, right):
    parts = split_faces(left * right)
    total = (parts[0] + parts[1]) + (parts[2] + parts[3]) + (parts[4] + parts[5])
    return matmul_nt_exact(jnp.ones((8, FACE), F32), total)


def living_kernel(counts, live_ref):
    live_ref[...] = jnp.full((8, FACE), (counts[0] > 0).astype(F32), F32)


def prepare_kernel(live_ref, loads, value_ref, *sends):
    mark = live_ref[...]
    value = loads[0] * mark[0:1, 0:1]
    value_ref[...] = value
    faces = [jnp.concatenate([face, mark], axis=0) for face in split_faces(value)]
    store_sends(sends, faces)


def stage_kernel(matrix, table, matrix_out, table_out):
    matrix_out[...] = matrix[...]
    table_out[...] = table[...]


def halves_kernel(source, after, out, whole, turned):
    for c in range(COARSE // FACE):
        whole[c] = source[:, c * FACE : (c + 1) * FACE]
    for i in range(2):
        for c in range(COARSE // FACE):
            part = whole[c, pl.Slice(i, DEVICES, 2), :].T
            for h in range(2):
                turned[h, c * FACE : (c + 1) * FACE, :] = part[:, h * FACE : (h + 1) * FACE]
        for j in range(2):
            for h in range(2):
                high, low = halves(turned[h, pl.Slice(j, DEVICES, 2), :])
                first, start = j * DEVICES, i * DEVICES + h * FACE
                out[0, first : first + DEVICES, start : start + FACE] = high
                out[1, first : first + DEVICES, start : start + FACE] = low


def precondition(weight, residual, dirichlet):
    scaled = (weight * residual).astype(BF16)
    return weight * matmul(scaled, dirichlet[0])


def first_kernel(live_ref, value_ref, pairing, dirichlet, *refs):
    recvs, (resid, weight_ref, terms, dots), sends = refs[:6], refs[6:10], refs[10:]
    live = live_ref[0:1, 0:1]
    residual = live * (value_ref[...] + partner(recvs, pairing))
    multiplicity = live * (live + partner(recvs, pairing, slice(LOADS, LOADS + 8)))
    weight = live / jnp.maximum(multiplicity, 1.0)
    weight_ref[...] = weight
    resid[...] = residual
    applied = precondition(weight[0:1], residual, dirichlet)
    terms[...] = applied
    dots[...] = load_sums(residual, applied)
    store_sends(sends, split_faces(applied))


def corner_message(corner_map, corner_terms, scalars):
    place = coords()
    steps = ((0, 0, 0), (0, 1, 0), (1, 0, 0), (0, -1, 0), (-1, 0, 0), (0, 0, 1), None, (0, 0, -1))
    row = lax.broadcasted_iota(jnp.int32, (16, FACE), 0)
    target = jnp.full((16, FACE), -1, jnp.int32)
    for index, step in enumerate(steps):
        if step is not None:
            a, b, c = [(p + s + n) % n for p, s, n in zip(place, step, SIZES)]
            owned = 2 * ((a * SIZES[1] + b) * SIZES[2] + c)
            target = jnp.where(row == index, owned, target)
            target = jnp.where(row == index + 8, owned + 1, target)
    chosen = (target == corner_map[0:1, :]).astype(F32)
    sums = matmul_nt_exact(chosen, corner_terms)
    line = lax.broadcasted_iota(jnp.int32, (8, LOADS), 0)
    pair = [
        jnp.where(line == 6, scalar, sums[8 * i : 8 * i + 8]) for i, scalar in enumerate(scalars)
    ]
    messages = []
    for k in range(2):
        part = jnp.concatenate([value[:, k * HALF : (k + 1) * HALF] for value in pair], axis=1)
        messages.append(jnp.concatenate([part[2 * i : 2 * i + 2] for i in range(4)], axis=1))
    return messages


def send_message(out, messages):
    block = jnp.concatenate(messages * 4, axis=0)
    for i in range(2 * DEVICES // 16):
        out[i * 16 : (i + 1) * 16] = block


def second_kernel(live_ref, pairing, corner_map, schur, coupling, terms, dots, *refs):
    recvs, (z_ref, local_ref, out) = refs[:6], refs[6:]
    live = live_ref[0:1, 0:1]
    direction = live * (terms[...] + partner(recvs, pairing))
    dir_bf = direction.astype(BF16)
    local_terms = live * matmul(dir_bf, schur[0])
    corner_terms = live * matmul(dir_bf, coupling[0])
    z_ref[...] = direction
    local_ref[...] = local_terms
    curve = load_sums(direction, local_terms)
    send_message(out, corner_message(corner_map, corner_terms, (dots[0:1], curve[0:1])))


BY_COLUMN = ("gy", "gz", "region")


def combine_kernel(got, out, scratch):
    total = jnp.zeros((8, FACE), F32)

    def line(b, c, index):
        first = (b % SIZES[1] * SIZES[2] + c % SIZES[2]) * SIZES[0]
        return got[pl.Slice(2 * first + index, SIZES[0], 2), :]

    for b in range(SIZES[1]):
        for c in range(SIZES[2]):
            here = line(b, c, 0)
            near = here + line(b - 1, c, 1)
            near = near + pltpu.roll(pltpu.roll(here, 1, 0) + line(b + 1, c, 1), 96, 1)
            near = near + pltpu.roll(pltpu.roll(here, 7, 0) + line(b, c - 1, 1), 64, 1)
            near = near + pltpu.roll(line(b, c + 1, 1), 32, 1)
            scratch[pl.Slice(b * SIZES[2] + c, SIZES[0], SIDE), :] = near
            total = total + here
    out[:, 0:DEVICES] = scratch[...].T[0:LOADS]
    scalars = jnp.broadcast_to(jnp.sum(total, axis=0, keepdims=True), (FACE, FACE)).T
    out[:, DEVICES : DEVICES + FACE] = scalars[96:128]


def coarse_sums(mine, other):
    odd = coords()[0] % 2 == 1
    low = jnp.where(odd, other[...], mine[...])
    high = jnp.where(odd, mine[...], other[...])
    both = [
        jnp.concatenate([low[i * HALF : (i + 1) * HALF], high[i * HALF : (i + 1) * HALF]], axis=0)
        for i in range(2)
    ]
    gathered = jnp.concatenate([value[:, 0:DEVICES] for value in both], axis=1)
    return gathered, [value[:, DEVICES : DEVICES + 1] for value in both]


def coarse_solve(inverse, gathered, corner_map, coupling):
    high, low = halves(gathered)
    both = matmul(jnp.concatenate([high, low], axis=0), inverse[0])
    solved = both[:LOADS] + (both[LOADS:] + matmul(high, inverse[1]))
    solved = solved.astype(BF16)
    row = lax.broadcasted_iota(jnp.int32, (COARSE, FACE), 0)
    index = corner_map[0:1, :]
    index = (index & 1) * DEVICES + (index >> 1)
    chosen = (row == index).astype(F32).astype(BF16)
    picked = matmul(solved, chosen).astype(BF16)
    return matmul_nt(picked, coupling[0]), solved.astype(F32)


def coarse_dot(solved, gathered):
    return jnp.sum(solved * gathered, axis=1, keepdims=True)


def lanes(*columns):
    lane = lax.broadcasted_iota(jnp.int32, (LOADS, FACE), 1)
    out = jnp.zeros((LOADS, FACE), F32)
    for index, value in enumerate(columns):
        out = jnp.where(lane == index, value, out)
    return out


def third_kernel(live_ref, corner_map, coupling, inverse, mine, other, local_ref, *refs):
    image_ref, gathered_ref, solved_ref, scalar_ref = refs[:4]
    sends = refs[4:]
    live = live_ref[0:1, 0:1]
    gathered, (resid_dot, local_curve) = coarse_sums(mine, other)
    coarse_terms, solved = coarse_solve(inverse, gathered, corner_map, coupling)
    image = live * (local_ref[...] + coarse_terms)
    curvature = local_curve + coarse_dot(solved, gathered)
    step_size = resid_dot / curvature
    image_ref[...] = image
    gathered_ref[...] = gathered
    solved_ref[...] = solved
    scalar_ref[...] = lanes(resid_dot, local_curve, step_size, curvature)
    store_sends(sends, split_faces(image))


def fourth_kernel(live_ref, pairing, dirichlet, resid, weight_ref, image_ref, scalar_ref, *refs):
    recvs, (resid_out, terms, dots), sends = refs[:6], refs[6:9], refs[9:]
    live = live_ref[0:1, 0:1]
    step_size = scalar_ref[:, 2:3]
    residual = resid[...] - step_size * (live * (image_ref[...] + partner(recvs, pairing)))
    resid_out[...] = residual
    applied = precondition(weight_ref[0:1, :], residual, dirichlet)
    terms[...] = applied
    dots[...] = load_sums(residual, applied)
    store_sends(sends, split_faces(applied))


def fifth_kernel(live_ref, pairing, corner_map, schur, coupling, terms, dots, *refs):
    recvs, (precond_ref, out) = refs[:6], refs[6:]
    live = live_ref[0:1, 0:1]
    precond = live * (terms[...] + partner(recvs, pairing))
    precond_ref[...] = precond
    high, low = halves(precond)
    local_terms = live * matmul(high, schur[0])
    both = matmul(jnp.concatenate([high, low], axis=0), coupling[0])
    corner_terms = live * (both[:LOADS] + both[LOADS:])
    square = load_sums(precond, local_terms)
    send_message(out, corner_message(corner_map, corner_terms, (dots[0:1], square[0:1])))


def sixth_kernel(
    live_ref, corner_map, schur, coupling, inverse, mine, other, gathered_ref, solved_ref,
    scalar_ref, z_ref, precond_ref, *refs
):
    direction_ref, image_ref, step_ref = refs[:3]
    sends = refs[3:]
    live = live_ref[0:1, 0:1]
    gathered, (new_dot, square) = coarse_sums(mine, other)
    beta = new_dot / scalar_ref[:, 0:1]
    cross = -beta * scalar_ref[:, 3:4] - coarse_dot(solved_ref[...], gathered)
    gathered = gathered + beta * gathered_ref[...]
    coarse_terms, solved = coarse_solve(inverse, gathered, corner_map, coupling)
    local_curve = square + beta * (2.0 * cross + beta * scalar_ref[:, 1:2])
    step_size = new_dot / (local_curve + coarse_dot(solved, gathered))
    first = z_ref[...]
    direction = precond_ref[...] + beta * first
    local_terms = matmul(direction.astype(BF16), schur[0])
    image = live * (local_terms + coarse_terms)
    image_ref[...] = image
    store_sends(sends, split_faces(image))
    step_ref[...] = lanes(step_size)
    direction_ref[...] = direction


def solution_kernel(scalar_ref, first, step_ref, direction, out):
    out[0] = scalar_ref[:, 2:3] * first[...] + step_ref[:, 0:1] * direction[...]


def seventh_kernel(live_ref, pairing, resid, image_ref, step_ref, *refs):
    recvs, (out,) = refs[:6], refs[6:]
    live = live_ref[0:1, 0:1]
    image = live * (image_ref[...] + partner(recvs, pairing))
    out[0] = resid[...] - step_ref[:, 0:1] * image


def call(kernel, shapes, *operands, scratch=(), cost=None, spec=VM):
    return pl.pallas_call(
        kernel,
        out_shape=[
            shape if hasattr(shape, "dtype") else jax.ShapeDtypeStruct(shape, F32)
            for shape in shapes
        ],
        in_specs=[spec] * len(operands),
        out_specs=[VM] * len(shapes),
        scratch_shapes=list(scratch),
        cost_estimate=cost,
        compiler_params=pltpu.CompilerParams(vmem_limit_bytes=32 << 20),
    )(*operands)


def pairs(axis, start):
    out = []
    for a in range(SIZES[0]):
        for b in range(SIZES[1]):
            for c in range(SIZES[2]):
                here, there = (a, b, c), [a, b, c]
                if start and here[axis] in (0, SIZES[axis] - 1):
                    other = 1 if axis == 0 else 0
                    there[other] = here[other] ^ 1
                else:
                    there[axis] += 1 if (here[axis] - start) % 2 == 0 else -1
                place = [(p * SIZES[1] + q) * SIZES[2] + r for p, q, r in (here, there)]
                out.append(tuple(place))
    return out


def exchange(sends):
    return [
        lax.ppermute(value, AXES, pairs(k // 2, k % 2)) for k, value in zip(ORDER, sends)
    ]


def total_sums(message):
    message = lax.all_to_all(message.reshape(DEVICES, 2, FACE), BY_COLUMN, 0, 0)
    (mine,) = call(
        combine_kernel, [(LOADS, DEVICES + FACE)], message.reshape(2 * DEVICES, FACE),
        scratch=[pltpu.VMEM((DEVICES, FACE), F32)],
    )
    return mine, lax.ppermute(mine, AXES, pairs(0, 0))


def local(loads, schur, dirichlet, coupling, coarse_inverse, pairing, corner_map, counts):
    vector = (LOADS, MULT)
    faces = [(LOADS, FACE)] * 6
    small = (8, LOADS)
    wide = (LOADS, FACE)

    pairing = pairing.reshape(6, 1, FACE)
    cost = pl.CostEstimate(flops=0, bytes_accessed=4 << 20, transcendentals=0)
    (live,) = call(living_kernel, [(8, FACE)], counts, spec=SMEM, cost=cost)
    value, *sends = call(prepare_kernel, [vector] + [(LOADS + 8, FACE)] * 6, live, loads)
    dirichlet, pairing = call(
        stage_kernel,
        [jax.ShapeDtypeStruct(x.shape, x.dtype) for x in (dirichlet, pairing)],
        dirichlet, pairing,
    )
    resid, weight, terms, dots, *sends = call(
        first_kernel, [vector, (8, MULT), vector, small] + faces,
        live, value, pairing, dirichlet, *exchange(sends),
    )
    (inverse,) = call(
        halves_kernel, [jax.ShapeDtypeStruct((2, COARSE, COARSE), BF16)], coarse_inverse, dots,
        scratch=[
            pltpu.VMEM((COARSE // FACE, COARSE, FACE), F32),
            pltpu.VMEM((2, COARSE, FACE), F32),
        ],
    )
    first, local_terms, message = call(
        second_kernel, [vector, vector, (2 * DEVICES, FACE)],
        live, pairing, corner_map, schur, coupling, terms, dots, *exchange(sends),
    )
    image, gathered, solved, scalars, *sends = call(
        third_kernel, [vector, (LOADS, COARSE), (LOADS, COARSE), wide] + faces,
        live, corner_map, coupling, inverse, *total_sums(message), local_terms,
    )
    resid, terms, dots, *sends = call(
        fourth_kernel, [vector, vector, small] + faces,
        live, pairing, dirichlet, resid, weight, image, scalars, *exchange(sends),
    )
    precond, message = call(
        fifth_kernel, [vector, (2 * DEVICES, FACE)],
        live, pairing, corner_map, schur, coupling, terms, dots, *exchange(sends),
    )
    direction, image, step, *sends = call(
        sixth_kernel, [vector, vector, wide] + faces,
        live, corner_map, schur, coupling, inverse, *total_sums(message),
        gathered, solved, scalars, first, precond,
    )
    (solution_out,) = call(solution_kernel, [(1,) + vector], scalars, first, step, direction)
    (residual_out,) = call(
        seventh_kernel, [(1,) + vector],
        live, pairing, resid, image, step, *exchange(sends),
    )
    return solution_out, residual_out


def solution(mesh):
    block = P(AXES, None, None)
    in_specs = (block, block, block, block, P(), block, P(AXES, None), P(AXES))
    return jax.shard_map(
        local, mesh=mesh, in_specs=in_specs, out_specs=(block, block), check_vma=False
    )
```

```python
import jax
import jax.numpy as jnp
from jax import lax
from jax.experimental import pallas as pl
from jax.experimental.pallas import tpu as pltpu
from jax.sharding import PartitionSpec as P

AXES = ("region", "gy", "gz")
SIZES = (8, 8, 4)
F32 = jnp.float32
BF16 = jnp.bfloat16
LOADS = 32
FACE = 128
MULT = 768
COARSE = 512
SIDE = 32
HALF = 16
DEVICES = 256
HIGHEST = lax.Precision.HIGHEST
VM = pl.BlockSpec(memory_space=pltpu.VMEM)
SMEM = pl.BlockSpec(memory_space=pltpu.SMEM)


def matmul(left, right):
    return jnp.dot(left, right, preferred_element_type=F32)


def halves(value):
    high = value.astype(BF16)
    return high, (value - high.astype(F32)).astype(BF16)


def matmul_nt(left, right):
    return lax.dot_general(left, right, (((1,), (1,)), ((), ())), preferred_element_type=F32)


def coords():
    return [lax.axis_index(axis) for axis in AXES]


ORDER = (3, 2, 1, 4, 5, 0)


def store_sends(sends, faces):
    for e, place in enumerate(coords()):
        odd = place % 2 == 1
        first, second = ORDER.index(2 * e), ORDER.index(2 * e + 1)
        sends[first][...] = jnp.where(odd, faces[2 * e], faces[2 * e + 1])
        sends[second][...] = jnp.where(odd, faces[2 * e + 1], faces[2 * e])


def received_faces(recvs, rows):
    out = []
    for e, place in enumerate(coords()):
        odd = place % 2 == 1
        first = recvs[ORDER.index(2 * e)][rows, :]
        second = recvs[ORDER.index(2 * e + 1)][rows, :]
        lower = jnp.where(odd, first, second)
        upper = jnp.where(odd, second, first)
        out.append(jnp.where(place > 0, lower, 0.0))
        out.append(jnp.where(place < SIZES[e] - 1, upper, 0.0))
    return out


def partner(recvs, pairing, rows=slice(0, LOADS)):
    faces = received_faces(recvs, rows)
    parts = []
    for f in range(6):
        index = jnp.broadcast_to(pairing[f], faces[f].shape)
        parts.append(jnp.take_along_axis(faces[f], index, axis=1))
    return jnp.concatenate(parts, axis=1)


def split_faces(value):
    return [value[:, f * FACE : (f + 1) * FACE] for f in range(6)]


def matmul_nt_exact(left, right):
    return lax.dot_general(
        left, right, (((1,), (1,)), ((), ())), precision=HIGHEST, preferred_element_type=F32
    )


def load_sums(left, right):
    parts = split_faces(left * right)
    total = (parts[0] + parts[1]) + (parts[2] + parts[3]) + (parts[4] + parts[5])
    return matmul_nt_exact(jnp.ones((8, FACE), F32), total)


def living_kernel(counts, live_ref):
    live_ref[...] = jnp.full((8, FACE), (counts[0] > 0).astype(F32), F32)


def prepare_kernel(live_ref, loads, value_ref, *sends):
    mark = live_ref[...]
    value = loads[0] * mark[0:1, 0:1]
    value_ref[...] = value
    faces = [jnp.concatenate([face, mark], axis=0) for face in split_faces(value)]
    store_sends(sends, faces)


def copy_kernel(source, out):
    out[...] = source[...]


def halves_kernel(source, after, out, whole, turned):
    for c in range(COARSE // FACE):
        whole[c] = source[:, c * FACE : (c + 1) * FACE]
    for i in range(2):
        for c in range(COARSE // FACE):
            part = whole[c, pl.Slice(i, DEVICES, 2), :].T
            for h in range(2):
                turned[h, c * FACE : (c + 1) * FACE, :] = part[:, h * FACE : (h + 1) * FACE]
        for j in range(2):
            for h in range(2):
                high, low = halves(turned[h, pl.Slice(j, DEVICES, 2), :])
                first, start = j * DEVICES, i * DEVICES + h * FACE
                out[0, first : first + DEVICES, start : start + FACE] = high
                out[1, first : first + DEVICES, start : start + FACE] = low


def precondition(weight, residual, dirichlet):
    scaled = (weight * residual).astype(BF16)
    return weight * matmul(scaled, dirichlet[0])


def first_kernel(live_ref, value_ref, pairing, dirichlet, *refs):
    recvs, (resid, weight_ref, terms, dots), sends = refs[:6], refs[6:10], refs[10:]
    live = live_ref[0:1, 0:1]
    residual = live * (value_ref[...] + partner(recvs, pairing))
    multiplicity = live * (live + partner(recvs, pairing, slice(LOADS, LOADS + 8)))
    weight = live / jnp.maximum(multiplicity, 1.0)
    weight_ref[...] = weight
    resid[...] = residual
    applied = precondition(weight[0:1], residual, dirichlet)
    terms[...] = applied
    dots[...] = load_sums(residual, applied)
    store_sends(sends, split_faces(applied))


def corner_message(corner_map, corner_terms, scalars):
    place = coords()
    steps = ((0, 0, 0), (0, 1, 0), (1, 0, 0), (0, -1, 0), (-1, 0, 0), (0, 0, 1), None, (0, 0, -1))
    row = lax.broadcasted_iota(jnp.int32, (16, FACE), 0)
    target = jnp.full((16, FACE), -1, jnp.int32)
    for index, step in enumerate(steps):
        if step is not None:
            a, b, c = [(p + s + n) % n for p, s, n in zip(place, step, SIZES)]
            owned = 2 * ((a * SIZES[1] + b) * SIZES[2] + c)
            target = jnp.where(row == index, owned, target)
            target = jnp.where(row == index + 8, owned + 1, target)
    chosen = (target == corner_map[0:1, :]).astype(F32)
    sums = matmul_nt_exact(chosen, corner_terms)
    line = lax.broadcasted_iota(jnp.int32, (8, LOADS), 0)
    pair = [
        jnp.where(line == 6, scalar, sums[8 * i : 8 * i + 8]) for i, scalar in enumerate(scalars)
    ]
    messages = []
    for k in range(2):
        part = jnp.concatenate([value[:, k * HALF : (k + 1) * HALF] for value in pair], axis=1)
        messages.append(jnp.concatenate([part[2 * i : 2 * i + 2] for i in range(4)], axis=1))
    return messages


def send_message(out, messages):
    block = jnp.concatenate(messages * 4, axis=0)
    for i in range(2 * DEVICES // 16):
        out[i * 16 : (i + 1) * 16] = block


def second_kernel(live_ref, pairing, corner_map, schur, coupling, terms, dots, *refs):
    recvs, (z_ref, local_ref, out) = refs[:6], refs[6:]
    live = live_ref[0:1, 0:1]
    direction = live * (terms[...] + partner(recvs, pairing))
    dir_bf = direction.astype(BF16)
    local_terms = live * matmul(dir_bf, schur[0])
    corner_terms = live * matmul(dir_bf, coupling[0])
    z_ref[...] = direction
    local_ref[...] = local_terms
    curve = load_sums(direction, local_terms)
    send_message(out, corner_message(corner_map, corner_terms, (dots[0:1], curve[0:1])))


BY_COLUMN = ("gy", "gz", "region")


def combine_kernel(got, out, scratch):
    total = jnp.zeros((8, FACE), F32)

    def line(b, c, index):
        first = (b % SIZES[1] * SIZES[2] + c % SIZES[2]) * SIZES[0]
        return got[pl.Slice(2 * first + index, SIZES[0], 2), :]

    for b in range(SIZES[1]):
        for c in range(SIZES[2]):
            here = line(b, c, 0)
            near = here + line(b - 1, c, 1)
            near = near + pltpu.roll(pltpu.roll(here, 1, 0) + line(b + 1, c, 1), 96, 1)
            near = near + pltpu.roll(pltpu.roll(here, 7, 0) + line(b, c - 1, 1), 64, 1)
            near = near + pltpu.roll(line(b, c + 1, 1), 32, 1)
            scratch[pl.Slice(b * SIZES[2] + c, SIZES[0], SIDE), :] = near
            total = total + here
    out[:, 0:DEVICES] = scratch[...].T[0:LOADS]
    scalars = jnp.broadcast_to(jnp.sum(total, axis=0, keepdims=True), (FACE, FACE)).T
    out[:, DEVICES : DEVICES + FACE] = scalars[96:128]


def coarse_sums(mine, other):
    odd = coords()[0] % 2 == 1
    low = jnp.where(odd, other[...], mine[...])
    high = jnp.where(odd, mine[...], other[...])
    both = [
        jnp.concatenate([low[i * HALF : (i + 1) * HALF], high[i * HALF : (i + 1) * HALF]], axis=0)
        for i in range(2)
    ]
    gathered = jnp.concatenate([value[:, 0:DEVICES] for value in both], axis=1)
    return gathered, [value[:, DEVICES : DEVICES + 1] for value in both]


def coarse_solve(inverse, gathered, corner_map, coupling):
    high, low = halves(gathered)
    both = matmul(jnp.concatenate([high, low], axis=0), inverse[0])
    solved = both[:LOADS] + (both[LOADS:] + matmul(high, inverse[1]))
    solved = solved.astype(BF16)
    row = lax.broadcasted_iota(jnp.int32, (COARSE, FACE), 0)
    index = corner_map[0:1, :]
    index = (index & 1) * DEVICES + (index >> 1)
    chosen = (row == index).astype(F32).astype(BF16)
    picked = matmul(solved, chosen).astype(BF16)
    return matmul_nt(picked, coupling[0]), solved.astype(F32)


def coarse_dot(solved, gathered):
    return jnp.sum(solved * gathered, axis=1, keepdims=True)


def lanes(*columns):
    lane = lax.broadcasted_iota(jnp.int32, (LOADS, FACE), 1)
    out = jnp.zeros((LOADS, FACE), F32)
    for index, value in enumerate(columns):
        out = jnp.where(lane == index, value, out)
    return out


def third_kernel(live_ref, corner_map, coupling, inverse, mine, other, local_ref, *refs):
    image_ref, gathered_ref, solved_ref, scalar_ref = refs[:4]
    sends = refs[4:]
    live = live_ref[0:1, 0:1]
    gathered, (resid_dot, local_curve) = coarse_sums(mine, other)
    coarse_terms, solved = coarse_solve(inverse, gathered, corner_map, coupling)
    image = live * (local_ref[...] + coarse_terms)
    curvature = local_curve + coarse_dot(solved, gathered)
    step_size = resid_dot / curvature
    image_ref[...] = image
    gathered_ref[...] = gathered
    solved_ref[...] = solved
    scalar_ref[...] = lanes(resid_dot, local_curve, step_size, curvature)
    store_sends(sends, split_faces(image))


def fourth_kernel(live_ref, pairing, dirichlet, resid, weight_ref, image_ref, scalar_ref, *refs):
    recvs, (resid_out, terms, dots), sends = refs[:6], refs[6:9], refs[9:]
    live = live_ref[0:1, 0:1]
    step_size = scalar_ref[:, 2:3]
    residual = resid[...] - step_size * (live * (image_ref[...] + partner(recvs, pairing)))
    resid_out[...] = residual
    applied = precondition(weight_ref[0:1, :], residual, dirichlet)
    terms[...] = applied
    dots[...] = load_sums(residual, applied)
    store_sends(sends, split_faces(applied))


def fifth_kernel(live_ref, pairing, corner_map, schur, coupling, terms, dots, *refs):
    recvs, (precond_ref, out) = refs[:6], refs[6:]
    live = live_ref[0:1, 0:1]
    precond = live * (terms[...] + partner(recvs, pairing))
    precond_ref[...] = precond
    high, low = halves(precond)
    local_terms = live * matmul(high, schur[0])
    both = matmul(jnp.concatenate([high, low], axis=0), coupling[0])
    corner_terms = live * (both[:LOADS] + both[LOADS:])
    square = load_sums(precond, local_terms)
    send_message(out, corner_message(corner_map, corner_terms, (dots[0:1], square[0:1])))


def sixth_kernel(
    live_ref, corner_map, schur, coupling, inverse, mine, other, gathered_ref, solved_ref,
    scalar_ref, z_ref, precond_ref, *refs
):
    direction_ref, image_ref, step_ref = refs[:3]
    sends = refs[3:]
    live = live_ref[0:1, 0:1]
    gathered, (new_dot, square) = coarse_sums(mine, other)
    beta = new_dot / scalar_ref[:, 0:1]
    cross = -beta * scalar_ref[:, 3:4] - coarse_dot(solved_ref[...], gathered)
    gathered = gathered + beta * gathered_ref[...]
    coarse_terms, solved = coarse_solve(inverse, gathered, corner_map, coupling)
    local_curve = square + beta * (2.0 * cross + beta * scalar_ref[:, 1:2])
    step_size = new_dot / (local_curve + coarse_dot(solved, gathered))
    first = z_ref[...]
    direction = precond_ref[...] + beta * first
    local_terms = matmul(direction.astype(BF16), schur[0])
    image = live * (local_terms + coarse_terms)
    image_ref[...] = image
    store_sends(sends, split_faces(image))
    step_ref[...] = lanes(step_size)
    direction_ref[...] = direction


def seventh_kernel(
    live_ref, pairing, resid, image_ref, scalar_ref, step_ref, first, direction, *refs
):
    recvs, (solution_ref, out) = refs[:6], refs[6:]
    solution_ref[0] = scalar_ref[:, 2:3] * first[...] + step_ref[:, 0:1] * direction[...]
    live = live_ref[0:1, 0:1]
    image = live * (image_ref[...] + partner(recvs, pairing))
    out[0] = resid[...] - step_ref[:, 0:1] * image


def call(kernel, shapes, *operands, scratch=(), cost=None, spec=VM):
    return pl.pallas_call(
        kernel,
        out_shape=[
            shape if hasattr(shape, "dtype") else jax.ShapeDtypeStruct(shape, F32)
            for shape in shapes
        ],
        in_specs=[spec] * len(operands),
        out_specs=[VM] * len(shapes),
        scratch_shapes=list(scratch),
        cost_estimate=cost,
        compiler_params=pltpu.CompilerParams(vmem_limit_bytes=32 << 20),
    )(*operands)


def pairs(axis, start):
    out = []
    for a in range(SIZES[0]):
        for b in range(SIZES[1]):
            for c in range(SIZES[2]):
                here, there = (a, b, c), [a, b, c]
                if start and here[axis] in (0, SIZES[axis] - 1):
                    other = 1 if axis == 0 else 0
                    there[other] = here[other] ^ 1
                else:
                    there[axis] += 1 if (here[axis] - start) % 2 == 0 else -1
                place = [(p * SIZES[1] + q) * SIZES[2] + r for p, q, r in (here, there)]
                out.append(tuple(place))
    return out


def exchange(sends):
    return [
        lax.ppermute(value, AXES, pairs(k // 2, k % 2)) for k, value in zip(ORDER, sends)
    ]


def total_sums(message):
    message = lax.all_to_all(message.reshape(DEVICES, 2, FACE), BY_COLUMN, 0, 0)
    (mine,) = call(
        combine_kernel, [(LOADS, DEVICES + FACE)], message.reshape(2 * DEVICES, FACE),
        scratch=[pltpu.VMEM((DEVICES, FACE), F32)],
    )
    return mine, lax.ppermute(mine, AXES, pairs(0, 0))


def local(loads, schur, dirichlet, coupling, coarse_inverse, pairing, corner_map, counts):
    vector = (LOADS, MULT)
    faces = [(LOADS, FACE)] * 6
    small = (8, LOADS)
    wide = (LOADS, FACE)

    pairing = pairing.reshape(6, 1, FACE)
    cost = pl.CostEstimate(flops=0, bytes_accessed=4 << 20, transcendentals=0)
    (live,) = call(living_kernel, [(8, FACE)], counts, spec=SMEM, cost=cost)
    value, *sends = call(prepare_kernel, [vector] + [(LOADS + 8, FACE)] * 6, live, loads)
    (dirichlet,) = call(copy_kernel, [jax.ShapeDtypeStruct(dirichlet.shape, BF16)], dirichlet)
    resid, weight, terms, dots, *sends = call(
        first_kernel, [vector, (8, MULT), vector, small] + faces,
        live, value, pairing, dirichlet, *exchange(sends),
    )
    (inverse,) = call(
        halves_kernel, [jax.ShapeDtypeStruct((2, COARSE, COARSE), BF16)], coarse_inverse, dots,
        scratch=[
            pltpu.VMEM((COARSE // FACE, COARSE, FACE), F32),
            pltpu.VMEM((2, COARSE, FACE), F32),
        ],
    )
    first, local_terms, message = call(
        second_kernel, [vector, vector, (2 * DEVICES, FACE)],
        live, pairing, corner_map, schur, coupling, terms, dots, *exchange(sends),
    )
    image, gathered, solved, scalars, *sends = call(
        third_kernel, [vector, (LOADS, COARSE), (LOADS, COARSE), wide] + faces,
        live, corner_map, coupling, inverse, *total_sums(message), local_terms,
    )
    resid, terms, dots, *sends = call(
        fourth_kernel, [vector, vector, small] + faces,
        live, pairing, dirichlet, resid, weight, image, scalars, *exchange(sends),
    )
    precond, message = call(
        fifth_kernel, [vector, (2 * DEVICES, FACE)],
        live, pairing, corner_map, schur, coupling, terms, dots, *exchange(sends),
    )
    direction, image, step, *sends = call(
        sixth_kernel, [vector, vector, wide] + faces,
        live, corner_map, schur, coupling, inverse, *total_sums(message),
        gathered, solved, scalars, first, precond,
    )
    solution_out, residual_out = call(
        seventh_kernel, [(1,) + vector] * 2,
        live, pairing, resid, image, scalars, step, first, direction, *exchange(sends),
    )
    return solution_out, residual_out


def solution(mesh):
    block = P(AXES, None, None)
    in_specs = (block, block, block, block, P(), block, P(AXES, None), P(AXES))
    return jax.shard_map(
        local, mesh=mesh, in_specs=in_specs, out_specs=(block, block), check_vma=False
    )
```

```python
import jax
import jax.numpy as jnp
from jax import lax
from jax.experimental import pallas as pl
from jax.experimental.pallas import tpu as pltpu
from jax.sharding import PartitionSpec as P

AXES = ("region", "gy", "gz")
SIZES = (8, 8, 4)
F32 = jnp.float32
BF16 = jnp.bfloat16
LOADS = 32
FACE = 128
MULT = 768
COARSE = 512
SIDE = 32
HALF = 16
DEVICES = 256
HIGHEST = lax.Precision.HIGHEST
VM = pl.BlockSpec(memory_space=pltpu.VMEM)
SMEM = pl.BlockSpec(memory_space=pltpu.SMEM)


def matmul(left, right):
    return jnp.dot(left, right, preferred_element_type=F32)


def halves(value):
    high = value.astype(BF16)
    return high, (value - high.astype(F32)).astype(BF16)


def matmul_nt(left, right):
    return lax.dot_general(left, right, (((1,), (1,)), ((), ())), preferred_element_type=F32)


def coords():
    return [lax.axis_index(axis) for axis in AXES]


ORDER = (3, 2, 1, 4, 5, 0)


def store_sends(sends, faces):
    for e, place in enumerate(coords()):
        odd = place % 2 == 1
        first, second = ORDER.index(2 * e), ORDER.index(2 * e + 1)
        sends[first][...] = jnp.where(odd, faces[2 * e], faces[2 * e + 1])
        sends[second][...] = jnp.where(odd, faces[2 * e + 1], faces[2 * e])


def received_faces(recvs, rows):
    out = []
    for e, place in enumerate(coords()):
        odd = place % 2 == 1
        first = recvs[ORDER.index(2 * e)][rows, :]
        second = recvs[ORDER.index(2 * e + 1)][rows, :]
        lower = jnp.where(odd, first, second)
        upper = jnp.where(odd, second, first)
        out.append(jnp.where(place > 0, lower, 0.0))
        out.append(jnp.where(place < SIZES[e] - 1, upper, 0.0))
    return out


def partner(recvs, pairing, rows=slice(0, LOADS)):
    faces = received_faces(recvs, rows)
    parts = []
    for f in range(6):
        index = jnp.broadcast_to(pairing[f], faces[f].shape)
        parts.append(jnp.take_along_axis(faces[f], index, axis=1))
    return jnp.concatenate(parts, axis=1)


def split_faces(value):
    return [value[:, f * FACE : (f + 1) * FACE] for f in range(6)]


def matmul_nt_exact(left, right):
    return lax.dot_general(
        left, right, (((1,), (1,)), ((), ())), precision=HIGHEST, preferred_element_type=F32
    )


def load_sums(left, right):
    parts = split_faces(left * right)
    total = (parts[0] + parts[1]) + (parts[2] + parts[3]) + (parts[4] + parts[5])
    return jnp.broadcast_to(jnp.sum(total.T, axis=0, keepdims=True), (8, LOADS))


def living_kernel(counts, live_ref):
    live_ref[...] = jnp.full((8, FACE), (counts[0] > 0).astype(F32), F32)


def prepare_kernel(live_ref, loads, value_ref, *sends):
    mark = live_ref[...]
    value = loads[0] * mark[0:1, 0:1]
    value_ref[...] = value
    faces = [jnp.concatenate([face, mark], axis=0) for face in split_faces(value)]
    store_sends(sends, faces)


def copy_kernel(source, out):
    out[...] = source[...]


def halves_kernel(source, after, out, whole, turned):
    for c in range(COARSE // FACE):
        whole[c] = source[:, c * FACE : (c + 1) * FACE]
    for i in range(2):
        for c in range(COARSE // FACE):
            part = whole[c, pl.Slice(i, DEVICES, 2), :].T
            for h in range(2):
                turned[h, c * FACE : (c + 1) * FACE, :] = part[:, h * FACE : (h + 1) * FACE]
        for j in range(2):
            for h in range(2):
                high, low = halves(turned[h, pl.Slice(j, DEVICES, 2), :])
                first, start = j * DEVICES, i * DEVICES + h * FACE
                out[0, first : first + DEVICES, start : start + FACE] = high
                out[1, first : first + DEVICES, start : start + FACE] = low


def precondition(weight, residual, dirichlet):
    scaled = (weight * residual).astype(BF16)
    return weight * matmul(scaled, dirichlet[0])


def first_kernel(live_ref, value_ref, pairing, dirichlet, *refs):
    recvs, (resid, weight_ref, terms, dots), sends = refs[:6], refs[6:10], refs[10:]
    live = live_ref[0:1, 0:1]
    residual = live * (value_ref[...] + partner(recvs, pairing))
    multiplicity = live * (live + partner(recvs, pairing, slice(LOADS, LOADS + 8)))
    weight = live / jnp.maximum(multiplicity, 1.0)
    weight_ref[...] = weight
    resid[...] = residual
    applied = precondition(weight[0:1], residual, dirichlet)
    terms[...] = applied
    dots[...] = load_sums(residual, applied)
    store_sends(sends, split_faces(applied))


def corner_message(corner_map, corner_terms, scalars):
    place = coords()
    steps = ((0, 0, 0), (0, 1, 0), (1, 0, 0), (0, -1, 0), (-1, 0, 0), (0, 0, 1), None, (0, 0, -1))
    row = lax.broadcasted_iota(jnp.int32, (16, FACE), 0)
    target = jnp.full((16, FACE), -1, jnp.int32)
    for index, step in enumerate(steps):
        if step is not None:
            a, b, c = [(p + s + n) % n for p, s, n in zip(place, step, SIZES)]
            owned = 2 * ((a * SIZES[1] + b) * SIZES[2] + c)
            target = jnp.where(row == index, owned, target)
            target = jnp.where(row == index + 8, owned + 1, target)
    chosen = (target == corner_map[0:1, :]).astype(F32)
    sums = matmul_nt_exact(chosen, corner_terms)
    line = lax.broadcasted_iota(jnp.int32, (8, LOADS), 0)
    pair = [
        jnp.where(line == 6, scalar, sums[8 * i : 8 * i + 8]) for i, scalar in enumerate(scalars)
    ]
    messages = []
    for k in range(2):
        part = jnp.concatenate([value[:, k * HALF : (k + 1) * HALF] for value in pair], axis=1)
        messages.append(jnp.concatenate([part[2 * i : 2 * i + 2] for i in range(4)], axis=1))
    return messages


def send_message(out, messages):
    block = jnp.concatenate(messages * 4, axis=0)
    for i in range(2 * DEVICES // 16):
        out[i * 16 : (i + 1) * 16] = block


def second_kernel(live_ref, pairing, corner_map, schur, coupling, terms, dots, *refs):
    recvs, (z_ref, local_ref, out) = refs[:6], refs[6:]
    live = live_ref[0:1, 0:1]
    direction = live * (terms[...] + partner(recvs, pairing))
    dir_bf = direction.astype(BF16)
    local_terms = live * matmul(dir_bf, schur[0])
    corner_terms = live * matmul(dir_bf, coupling[0])
    z_ref[...] = direction
    local_ref[...] = local_terms
    curve = load_sums(direction, local_terms)
    send_message(out, corner_message(corner_map, corner_terms, (dots[0:1], curve[0:1])))


BY_COLUMN = ("gy", "gz", "region")


def combine_kernel(got, out, scratch):
    total = jnp.zeros((8, FACE), F32)

    def line(b, c, index):
        first = (b % SIZES[1] * SIZES[2] + c % SIZES[2]) * SIZES[0]
        return got[pl.Slice(2 * first + index, SIZES[0], 2), :]

    for b in range(SIZES[1]):
        for c in range(SIZES[2]):
            here = line(b, c, 0)
            near = here + line(b - 1, c, 1)
            near = near + pltpu.roll(pltpu.roll(here, 1, 0) + line(b + 1, c, 1), 96, 1)
            near = near + pltpu.roll(pltpu.roll(here, 7, 0) + line(b, c - 1, 1), 64, 1)
            near = near + pltpu.roll(line(b, c + 1, 1), 32, 1)
            scratch[pl.Slice(b * SIZES[2] + c, SIZES[0], SIDE), :] = near
            total = total + here
    out[:, 0:DEVICES] = scratch[...].T[0:LOADS]
    scalars = jnp.broadcast_to(jnp.sum(total, axis=0, keepdims=True), (FACE, FACE)).T
    out[:, DEVICES : DEVICES + FACE] = scalars[96:128]


def coarse_sums(mine, other):
    odd = coords()[0] % 2 == 1
    low = jnp.where(odd, other[...], mine[...])
    high = jnp.where(odd, mine[...], other[...])
    both = [
        jnp.concatenate([low[i * HALF : (i + 1) * HALF], high[i * HALF : (i + 1) * HALF]], axis=0)
        for i in range(2)
    ]
    gathered = jnp.concatenate([value[:, 0:DEVICES] for value in both], axis=1)
    return gathered, [value[:, DEVICES : DEVICES + 1] for value in both]


def coarse_solve(inverse, gathered, corner_map, coupling):
    high, low = halves(gathered)
    both = matmul(jnp.concatenate([high, low], axis=0), inverse[0])
    solved = both[:LOADS] + (both[LOADS:] + matmul(high, inverse[1]))
    solved = solved.astype(BF16)
    row = lax.broadcasted_iota(jnp.int32, (COARSE, FACE), 0)
    index = corner_map[0:1, :]
    index = (index & 1) * DEVICES + (index >> 1)
    chosen = (row == index).astype(F32).astype(BF16)
    picked = matmul(solved, chosen).astype(BF16)
    return matmul_nt(picked, coupling[0]), solved.astype(F32)


def coarse_dot(solved, gathered):
    return jnp.sum(solved * gathered, axis=1, keepdims=True)


def lanes(*columns):
    lane = lax.broadcasted_iota(jnp.int32, (LOADS, FACE), 1)
    out = jnp.zeros((LOADS, FACE), F32)
    for index, value in enumerate(columns):
        out = jnp.where(lane == index, value, out)
    return out


def third_kernel(live_ref, corner_map, coupling, inverse, mine, other, local_ref, *refs):
    image_ref, gathered_ref, solved_ref, scalar_ref = refs[:4]
    sends = refs[4:]
    live = live_ref[0:1, 0:1]
    gathered, (resid_dot, local_curve) = coarse_sums(mine, other)
    coarse_terms, solved = coarse_solve(inverse, gathered, corner_map, coupling)
    image = live * (local_ref[...] + coarse_terms)
    curvature = local_curve + coarse_dot(solved, gathered)
    step_size = resid_dot / curvature
    image_ref[...] = image
    gathered_ref[...] = gathered
    solved_ref[...] = solved
    scalar_ref[...] = lanes(resid_dot, local_curve, step_size, curvature)
    store_sends(sends, split_faces(image))


def fourth_kernel(live_ref, pairing, dirichlet, resid, weight_ref, image_ref, scalar_ref, *refs):
    recvs, (resid_out, terms, dots), sends = refs[:6], refs[6:9], refs[9:]
    live = live_ref[0:1, 0:1]
    step_size = scalar_ref[:, 2:3]
    residual = resid[...] - step_size * (live * (image_ref[...] + partner(recvs, pairing)))
    resid_out[...] = residual
    applied = precondition(weight_ref[0:1, :], residual, dirichlet)
    terms[...] = applied
    dots[...] = load_sums(residual, applied)
    store_sends(sends, split_faces(applied))


def fifth_kernel(live_ref, pairing, corner_map, schur, coupling, terms, dots, *refs):
    recvs, (precond_ref, out) = refs[:6], refs[6:]
    live = live_ref[0:1, 0:1]
    precond = live * (terms[...] + partner(recvs, pairing))
    precond_ref[...] = precond
    high, low = halves(precond)
    local_terms = live * matmul(high, schur[0])
    both = matmul(jnp.concatenate([high, low], axis=0), coupling[0])
    corner_terms = live * (both[:LOADS] + both[LOADS:])
    square = load_sums(precond, local_terms)
    send_message(out, corner_message(corner_map, corner_terms, (dots[0:1], square[0:1])))


def sixth_kernel(
    live_ref, corner_map, schur, coupling, inverse, mine, other, gathered_ref, solved_ref,
    scalar_ref, z_ref, precond_ref, *refs
):
    direction_ref, image_ref, step_ref = refs[:3]
    sends = refs[3:]
    live = live_ref[0:1, 0:1]
    gathered, (new_dot, square) = coarse_sums(mine, other)
    beta = new_dot / scalar_ref[:, 0:1]
    cross = -beta * scalar_ref[:, 3:4] - coarse_dot(solved_ref[...], gathered)
    gathered = gathered + beta * gathered_ref[...]
    coarse_terms, solved = coarse_solve(inverse, gathered, corner_map, coupling)
    local_curve = square + beta * (2.0 * cross + beta * scalar_ref[:, 1:2])
    step_size = new_dot / (local_curve + coarse_dot(solved, gathered))
    first = z_ref[...]
    direction = precond_ref[...] + beta * first
    local_terms = matmul(direction.astype(BF16), schur[0])
    image = live * (local_terms + coarse_terms)
    image_ref[...] = image
    store_sends(sends, split_faces(image))
    step_ref[...] = lanes(step_size)
    direction_ref[...] = direction


def seventh_kernel(
    live_ref, pairing, resid, image_ref, scalar_ref, step_ref, first, direction, *refs
):
    recvs, (solution_ref, out) = refs[:6], refs[6:]
    solution_ref[0] = scalar_ref[:, 2:3] * first[...] + step_ref[:, 0:1] * direction[...]
    live = live_ref[0:1, 0:1]
    image = live * (image_ref[...] + partner(recvs, pairing))
    out[0] = resid[...] - step_ref[:, 0:1] * image


def call(kernel, shapes, *operands, scratch=(), cost=None, spec=VM):
    return pl.pallas_call(
        kernel,
        out_shape=[
            shape if hasattr(shape, "dtype") else jax.ShapeDtypeStruct(shape, F32)
            for shape in shapes
        ],
        in_specs=[spec] * len(operands),
        out_specs=[VM] * len(shapes),
        scratch_shapes=list(scratch),
        cost_estimate=cost,
        compiler_params=pltpu.CompilerParams(vmem_limit_bytes=32 << 20),
    )(*operands)


def pairs(axis, start):
    out = []
    for a in range(SIZES[0]):
        for b in range(SIZES[1]):
            for c in range(SIZES[2]):
                here, there = (a, b, c), [a, b, c]
                if start and here[axis] in (0, SIZES[axis] - 1):
                    other = 1 if axis == 0 else 0
                    there[other] = here[other] ^ 1
                else:
                    there[axis] += 1 if (here[axis] - start) % 2 == 0 else -1
                place = [(p * SIZES[1] + q) * SIZES[2] + r for p, q, r in (here, there)]
                out.append(tuple(place))
    return out


def exchange(sends):
    return [
        lax.ppermute(value, AXES, pairs(k // 2, k % 2)) for k, value in zip(ORDER, sends)
    ]


def total_sums(message):
    message = lax.all_to_all(message.reshape(DEVICES, 2, FACE), BY_COLUMN, 0, 0)
    (mine,) = call(
        combine_kernel, [(LOADS, DEVICES + FACE)], message.reshape(2 * DEVICES, FACE),
        scratch=[pltpu.VMEM((DEVICES, FACE), F32)],
    )
    return mine, lax.ppermute(mine, AXES, pairs(0, 0))


def local(loads, schur, dirichlet, coupling, coarse_inverse, pairing, corner_map, counts):
    vector = (LOADS, MULT)
    faces = [(LOADS, FACE)] * 6
    small = (8, LOADS)
    wide = (LOADS, FACE)

    pairing = pairing.reshape(6, 1, FACE)
    cost = pl.CostEstimate(flops=0, bytes_accessed=4 << 20, transcendentals=0)
    (live,) = call(living_kernel, [(8, FACE)], counts, spec=SMEM, cost=cost)
    value, *sends = call(prepare_kernel, [vector] + [(LOADS + 8, FACE)] * 6, live, loads)
    (dirichlet,) = call(copy_kernel, [jax.ShapeDtypeStruct(dirichlet.shape, BF16)], dirichlet)
    resid, weight, terms, dots, *sends = call(
        first_kernel, [vector, (8, MULT), vector, small] + faces,
        live, value, pairing, dirichlet, *exchange(sends),
    )
    (inverse,) = call(
        halves_kernel, [jax.ShapeDtypeStruct((2, COARSE, COARSE), BF16)], coarse_inverse, dots,
        scratch=[
            pltpu.VMEM((COARSE // FACE, COARSE, FACE), F32),
            pltpu.VMEM((2, COARSE, FACE), F32),
        ],
    )
    first, local_terms, message = call(
        second_kernel, [vector, vector, (2 * DEVICES, FACE)],
        live, pairing, corner_map, schur, coupling, terms, dots, *exchange(sends),
    )
    image, gathered, solved, scalars, *sends = call(
        third_kernel, [vector, (LOADS, COARSE), (LOADS, COARSE), wide] + faces,
        live, corner_map, coupling, inverse, *total_sums(message), local_terms,
    )
    resid, terms, dots, *sends = call(
        fourth_kernel, [vector, vector, small] + faces,
        live, pairing, dirichlet, resid, weight, image, scalars, *exchange(sends),
    )
    precond, message = call(
        fifth_kernel, [vector, (2 * DEVICES, FACE)],
        live, pairing, corner_map, schur, coupling, terms, dots, *exchange(sends),
    )
    direction, image, step, *sends = call(
        sixth_kernel, [vector, vector, wide] + faces,
        live, corner_map, schur, coupling, inverse, *total_sums(message),
        gathered, solved, scalars, first, precond,
    )
    solution_out, residual_out = call(
        seventh_kernel, [(1,) + vector] * 2,
        live, pairing, resid, image, scalars, step, first, direction, *exchange(sends),
    )
    return solution_out, residual_out


def solution(mesh):
    block = P(AXES, None, None)
    in_specs = (block, block, block, block, P(), block, P(AXES, None), P(AXES))
    return jax.shard_map(
        local, mesh=mesh, in_specs=in_specs, out_specs=(block, block), check_vma=False
    )
```
